512 devices in a mesh: ctx: 64 (over x, z_lo, core), tp: 8 (over z_hi, y).
Axes of the slice: x: 4, y: 4, z: 16 (z_hi: 2, z_lo: 8; z = z_hi * 8 + z_lo), core: 2. Of those that a mesh axis runs over, the one named last changes fastest.
Arguments:
- tokens: bfloat16 [8192, 4096], P('ctx', 'tp'), may hold values from -6 to 6
- w_in: bfloat16 [4096, 3, 512], P('tp'), may hold values from -0.09375 to 0.09375
- grad_out: bfloat16 [8192, 512], P('ctx', 'tp'), may hold values from -6 to 6
- filters: float32 [8, 64, 8192], P('tp', 'ctx'), may hold values from -2 to 2
Outputs:
- input_grad: bfloat16 [8192, 4096], P('ctx', 'tp')
- weight_grad: float32 [512, 3, 4096], P('ctx', None, 'tp')
- filter_grad: float32 [8, 64, 8192], P('tp', 'ctx')
The draws below stay inside these ranges and needn't reach their ends.
All inputs are finite; a program needn't handle non-finite values.
Results may differ from the reference program's by a relative error of at most 0.025.
Values may be sent and summed in bfloat16 or wider, within the bound.
A program may use at most 64 MiB of HBM per device.

```python
import math
import jax
import jax.numpy as jnp
from jax import lax

D = 4096
C = 512
TOKENS = 8192
N_TP = 8


def draw_filters(key, part):
    key = jax.random.fold_in(key, 11)
    key_rate, key_fast, key_span, key_noise = jax.random.split(key, 4)
    shape = (N_TP, C // N_TP, 1)
    rate = jnp.exp(jax.random.uniform(key_rate, shape, jnp.float32, jnp.log(0.5), jnp.log(6.0)))
    fast = jax.random.uniform(key_fast, shape, jnp.float32) < 0.3
    span = jax.random.uniform(key_span, shape, jnp.float32, 30.0, 50.0)
    steps = jnp.arange(TOKENS, dtype=jnp.float32)[None, None, :]
    slow_env = jnp.exp(-rate * steps / TOKENS) * jnp.sqrt(2.0 * rate / TOKENS)
    fast_env = jnp.exp(-steps / span) * jnp.sqrt(2.0 / span)
    envelope = jnp.where(fast, fast_env, slow_env)
    noise = jax.random.normal(key_noise, (N_TP, C // N_TP, TOKENS), jnp.float32)
    return jnp.clip(envelope * noise, -2.0, 2.0)


def steps_of(stream_key, dims, cuts, smallest, largest):
    factor_of, own = 1.0, jax.random.fold_in(stream_key, 6)
    for position, blocks in cuts:
        draws = jnp.exp(jax.random.uniform(jax.random.fold_in(own, position), (blocks,), jnp.float32, smallest / len(cuts), largest / len(cuts)))
        factor_of = factor_of * jnp.repeat(draws, dims[position] // blocks).reshape([-1 if axis == position else 1 for axis in range(len(dims))])
    return factor_of


def bell_draw(own_key, dims, deviation, limit, pieces=(), kind=jnp.bfloat16):
    entries = deviation * jax.random.normal(own_key, dims, jnp.float32)
    if pieces:
        entries = entries * steps_of(own_key, dims, pieces, -0.22, 0.18)
    return jnp.clip(entries, -limit, limit).astype(kind)


def setup_inputs(seed: int = 0) -> dict:
    splits = jax.random.split(jax.random.key(seed), 5)
    tokens = bell_draw(splits[0], (TOKENS, D), 1.0, 6.0, ((0, 64), (1, 8)))
    w_in = bell_draw(splits[1], (D, 3, C), D ** -0.5, 0.09375, ((0, 8),))
    grad_out = bell_draw(splits[2], (TOKENS, C), 1.0, 6.0, ((0, 64), (1, 8)))
    filters = draw_filters(jax.random.fold_in(splits[4], 71), 0)
    return dict(tokens=tokens, w_in=w_in, grad_out=grad_out, filters=filters)


def channel_block(inputs):
    query, key_part, value, grad_out, filt = inputs
    length = query.shape[1]
    nfft = 2 * length
    mixed = key_part.astype(jnp.float32) * value.astype(jnp.float32)
    grad_y = grad_out.astype(jnp.float32) * query.astype(jnp.float32)
    mixed_f = jnp.fft.rfft(mixed, n=nfft)
    filt_f = jnp.fft.rfft(filt, n=nfft)
    grad_f = jnp.fft.rfft(grad_y, n=nfft)
    output = jnp.fft.irfft(filt_f * mixed_f, n=nfft)[:, :length]
    grad_mixed = jnp.fft.irfft(jnp.conj(filt_f) * grad_f, n=nfft)[:, :length]
    filt_grad = jnp.fft.irfft(jnp.conj(mixed_f) * grad_f, n=nfft)[:, :length]
    grad_query = (grad_out.astype(jnp.float32) * output).astype(jnp.bfloat16)
    grad_mixed_b = grad_mixed.astype(jnp.bfloat16)
    grad_key = (grad_mixed_b.astype(jnp.float32) * value.astype(jnp.float32)).astype(jnp.bfloat16)
    grad_value = (grad_mixed_b.astype(jnp.float32) * key_part.astype(jnp.float32)).astype(jnp.bfloat16)
    scaled = (filt_grad / math.sqrt(length)).astype(jnp.float32)
    return (grad_query, grad_key, grad_value, scaled)

def reference(tokens, w_in, grad_out, filters):
    length = TOKENS
    feat = D // N_TP
    total = jnp.zeros((length, 3 * C), jnp.float32)
    for block in range(N_TP):
        piece = tokens[:, block * feat:(block + 1) * feat]
        weights = w_in[block * feat:(block + 1) * feat].reshape(feat, 3 * C)
        part = jnp.dot(piece, weights, preferred_element_type=jnp.float32)
        total = total + lax.optimization_barrier(part.astype(jnp.bfloat16)).astype(jnp.float32)
    qkv = total.astype(jnp.bfloat16).reshape(length, 3, C)
    group = 64
    blocks = C // group

    def split_rows(arr):
        return arr.T.reshape(blocks, group, length)
    inputs = (split_rows(qkv[:, 0]), split_rows(qkv[:, 1]), split_rows(qkv[:, 2]), split_rows(grad_out), filters.reshape(blocks, group, length))
    grad_query, grad_key, grad_value, filt_grad = lax.map(channel_block, inputs)
    grad_qkv = jnp.stack([grad_query.reshape(C, length).T, grad_key.reshape(C, length).T, grad_value.reshape(C, length).T], axis=1)
    flat = grad_qkv.reshape(length, 3 * C)
    weight_grad = jnp.dot(flat.T, tokens, preferred_element_type=jnp.float32)
    weight_grad = (weight_grad / math.sqrt(length)).reshape(3, C, D).transpose(1, 0, 2)
    input_grad = jnp.dot(flat, w_in.reshape(D, 3 * C).T, preferred_element_type=jnp.float32).astype(jnp.bfloat16)
    return (input_grad, weight_grad, filt_grad.reshape(N_TP, C // N_TP, length))
```

```python
import math

import jax
import jax.numpy as jnp
import numpy as np
from jax import lax
from jax.experimental import pallas as pl
from jax.experimental.pallas import tpu as pltpu
from jax.sharding import PartitionSpec as P

LENGTH = 8192
POINTS = 2 * LENGTH
MESH = pl.DeviceIdType.MESH
F32, BF16 = jnp.float32, jnp.bfloat16
EXACT = lax.Precision.HIGHEST


def selection(outs, ins, pairs):
    matrix = np.zeros((outs, ins), np.float32)
    for row, column in pairs:
        matrix[row, column] = 1.0
    return matrix


def selections():
    def ctx(p, zl):
        return (p >> 1) * 16 + zl * 2 + (p & 1)

    eight = range(8)
    r2q = selection(256, 192, [(zl * 32 + i * 8 + p, i * 64 + ctx(p, zl)) for zl in eight for i in range(3) for p in eight])
    r2g = selection(256, 64, [(zl * 32 + 24 + p, ctx(p, zl)) for zl in eight for p in eight])
    r3 = selection(
        256,
        512,
        [(p * 32 + i * 8 + zl, zh * 256 + zl * 32 + i * 8 + p) for zh in range(2) for zl in eight for i in range(4) for p in eight],
    )
    r5 = selection(256, 192, [(zl * 32 + i * 8 + p, i * 64 + p * 8 + zl) for zl in eight for i in range(3) for p in eight])
    r6 = selection(384, 512, [(p * 48 + z * 3 + i, z * 32 + i * 8 + p) for z in range(16) for i in range(3) for p in eight])
    r8 = selection(192, 192, [(m * 48 + q * 12 + r, q * 48 + m * 12 + r) for m in range(4) for q in range(4) for r in range(12)])
    r9 = selection(
        384,
        384,
        [(i * 128 + zh * 64 + ctx(p, zl), p * 48 + zh * 24 + zl * 3 + i) for i in range(3) for zh in range(2) for zl in eight for p in eight],
    )
    return [m.astype(jnp.bfloat16) for m in (r2q, r2g, r3, r5, r6, r8, r9)]


def transforms():
    turn = 2.0 * math.pi
    natural = np.arange(64)
    moved = np.array([(p >> 1) * 16 + zl * 2 + (p & 1) for p in range(8) for zl in range(8)])
    k = np.arange(128)

    def first(rows):
        angle = turn * ((k[:, None] * rows[None, :]) % 128) / 128
        return np.concatenate([np.cos(angle), -np.sin(angle)], 0)

    def last(rows, scale):
        angle = turn * ((rows[:, None] * k[None, :]) % 128) / 128
        return np.concatenate([np.cos(angle), -np.sin(angle)], 1) * scale

    angle = turn * (k[:, None] * k[None, :]) / POINTS
    twist = (np.cos(angle), -np.sin(angle))
    angle = turn * ((k[:, None] * k[None, :]) % 128) / 128
    c, s = np.cos(angle), np.sin(angle)
    forward = np.block([[c, -s], [s, c]])
    back = np.block([[c, s], [-s, c]])
    tables = (
        first(moved),
        first(natural),
        *twist,
        forward,
        back,
        last(moved, 1.0 / POINTS),
        last(natural, 1.0 / (POINTS * math.sqrt(LENGTH))),
    )
    return [t.astype(np.float32) for t in tables]


def dot(left, right, precision=None):
    return jnp.dot(left, right, precision=precision, preferred_element_type=F32)


def kernel(
    tok, w, go, filt,
    r2q, r2g, r3, r5, r6, r8, r9,
    f1p, f1n, twr, twi, mf, mi, g1p, g1n,
    ig_out, wg_out, fg_out,
    part, recv1, send2, recv2, send3, recv3, send5, recv5, recv6, recv7, send8, recv8, toks, gnat,
    s1, t1, s2, t2, s3, t3, s5, t5, s6, t6, s7, t7, s8, t8, sx, tx, sc, tc,
):
    k, j = lax.axis_index("ctx"), lax.axis_index("tp")
    x, zl, core = k // 16, (k // 2) % 8, k % 2
    zh, y = j // 4, j % 4
    z, p = zh * 8 + zl, x * 2 + core

    def at(x_, zl_, core_, zh_, y_):
        return (x_ * 16 + zl_ * 2 + core_, zh_ * 4 + y_)

    def at_y(y_):
        return at(x, zl, core, zh, y_)

    def at_z(z_):
        return at(x, z_ % 8, core, z_ // 8, y)

    def at_p(p_):
        return at(p_ // 2, zl, p_ % 2, zh, y)

    def target8(m):
        return at(((m // 2) % 2) * 2 + m // 8, ((m // 4) % 2) * 4 + x, m % 2, zh, y)

    def source8(s):
        return at(zl % 4, s % 8, s // 8, zh, y)

    own8 = zl % 4 == x
    own_m = ((x % 2) * 2 + zl // 4) * 4 + (x // 2) * 2 + core

    def each(low, high, body):
        def step(n, carry):
            body(n)
            return carry

        lax.fori_loop(low, high, step, 0)

    def send(src, dst, s, t, to):
        pltpu.make_async_remote_copy(
            src_ref=src, dst_ref=dst, send_sem=s, recv_sem=t, device_id=to, device_id_type=MESH
        ).start()

    def take(ref, sem):
        pltpu.make_async_copy(ref, ref, sem).wait()

    barrier = pltpu.get_barrier_semaphore()

    def greet(to):
        pl.semaphore_signal(barrier, inc=1, device_id=to, device_id_type=MESH)

    each(1, 4, lambda n: greet(at_y((y + n) % 4)))
    each(1, 16, lambda n: greet(at_z((z + n) % 16)))
    each(1, 8, lambda n: greet(at_p((p + n) % 8)))

    def greet8(s):
        @pl.when(jnp.logical_not(jnp.logical_and(own8, s == core * 8 + zl)))
        def _():
            greet(source8(s))

    each(0, 16, greet8)

    for i in range(3):
        rows = dot(tok[...], w[i]).T.astype(BF16)
        for h in range(2):
            for yy in range(4):
                first = (h * 4 + yy) * 64
                part[yy, i * 128 + h * 64 : i * 128 + h * 64 + 64, :] = rows[first : first + 64]
    toks[p] = tok[...]

    pl.semaphore_wait(barrier, 25 + jnp.where(own8, 15, 16))

    for n in range(1, 4):
        to = (y + n) % 4
        send(part.at[to], recv1.at[n - 1], s1, t1, at_y(to))
    each(1, 4, lambda n: send(tok, toks.at[p], sx, tx, at_p((p + 2 * n) % 8)))
    sibling = x * 2 + (1 - core)
    send(tok, toks.at[p], sc, tc, at_p(sibling))

    twist_r, twist_i = twr[...], twi[...]

    def spectrum(table, rows, count):
        a = dot(table[...], rows, EXACT)
        ar, ai = a[:128], a[128:]
        pieces = []
        for n in range(count):
            br, bi = ar[:, n * 128 : n * 128 + 128], ai[:, n * 128 : n * 128 + 128]
            pieces.append(jnp.concatenate([br * twist_r - bi * twist_i, br * twist_i + bi * twist_r], axis=1))
        return dot(jnp.concatenate(pieces, axis=0), mf[...], EXACT)

    def inverse(spectra):
        d = dot(jnp.concatenate(spectra, axis=0), mi[...], EXACT)
        reals, imags = [], []
        for n in range(len(spectra)):
            dr, di = d[n * 128 : n * 128 + 128, :128], d[n * 128 : n * 128 + 128, 128:]
            reals.append(dr * twist_r + di * twist_i)
            imags.append(di * twist_r - dr * twist_i)
        return jnp.concatenate([jnp.concatenate(reals, axis=1), jnp.concatenate(imags, axis=1)], axis=0)

    filt_f = spectrum(f1n, filt[...], 1)
    filt_r, filt_i = filt_f[:, :128], filt_f[:, 128:]
    cotangent = dot(r2g[...], go[...])

    take(recv1, t1)
    total = part[y].astype(F32)
    for n in range(3):
        total = total + recv1[n].astype(F32)
    total = total.astype(BF16)
    for h in range(2):
        rows = jnp.concatenate([total[i * 128 + h * 64 : i * 128 + h * 64 + 64] for i in range(3)], axis=0)
        moved = dot(r2q[...], rows) + cotangent * jnp.where(zh == h, 1.0, 0.0)
        send2[h * 8 : h * 8 + 8] = moved.astype(BF16).reshape(8, 32, 128)

    def to_z(buffer, dst, s, t, slab):
        def body(n):
            to = (z + n) % 16
            send(buffer.at[slab(to)], dst.at[z], s, t, at_z(to))

        each(1, 16, body)

    to_z(send2, recv2, s2, t2, lambda to: to)
    recv2[z] = send2[z]

    take(toks.at[pl.ds(0, 3)], tx)

    def forward(n):
        block = (p + 2 * n) % 8
        send(toks.at[block], toks.at[block], sc, tc, at_p(sibling))

    each(1, 4, forward)

    take(recv2.at[pl.ds(0, 15)], t2)
    moved = dot(r3[...], recv2[...].reshape(512, 128))
    send3[...] = moved.astype(BF16).reshape(8, 32, 128)

    def to_p3(n):
        to = (p + n) % 8
        send(send3.at[to], recv3.at[p], s3, t3, at_p(to))

    each(1, 8, to_p3)
    recv3[p] = send3[p]
    take(recv3.at[pl.ds(0, 7)], t3)

    lines = recv3[...].astype(F32).reshape(8, 4, 8, 128)
    query, key_part, value, cot = [lines[:, i].reshape(64, 128) for i in range(4)]
    spectra = spectrum(f1p, jnp.concatenate([key_part * value, cot * query], axis=1), 2)
    mix_r, mix_i = spectra[:128, :128], spectra[:128, 128:]
    grad_r, grad_i = spectra[128:, :128], spectra[128:, 128:]
    out_f = jnp.concatenate([filt_r * mix_r - filt_i * mix_i, filt_r * mix_i + filt_i * mix_r], axis=1)
    back_f = jnp.concatenate([filt_r * grad_r + filt_i * grad_i, filt_r * grad_i - filt_i * grad_r], axis=1)
    both = dot(g1p[...], inverse([out_f, back_f]), EXACT)
    grad_query = (cot * both[:, :128]).astype(BF16)
    grad_mixed = both[:, 128:].astype(BF16).astype(F32)
    grad_key = (grad_mixed * value).astype(BF16)
    grad_value = (grad_mixed * key_part).astype(BF16)

    rows = jnp.concatenate([grad_query, grad_key, grad_value], axis=0)
    send5[...] = dot(r5[...], rows).astype(BF16).reshape(8, 32, 128)
    to_z(send5, recv5, s5, t5, lambda to: to % 8)
    recv5[z] = send5[zl]

    filt_f = jnp.concatenate([mix_r * grad_r + mix_i * grad_i, mix_r * grad_i - mix_i * grad_r], axis=1)
    fg_out[...] = dot(g1n[...], inverse([filt_f]), EXACT)

    take(recv5.at[pl.ds(0, 15)], t5)
    moved = dot(r6[...], recv5[...].reshape(512, 128))
    recv6[y] = moved.astype(BF16).reshape(8, 48, 128)
    for n in range(1, 4):
        send(recv6.at[y], recv6.at[y], s6, t6.at[4 - n], at_y((y + n) % 4))

    take(toks.at[pl.ds(0, 4)], tc)
    for n in range(4):
        yy = (y + n) % 4
        if n > 0:
            take(recv6.at[yy], t6.at[n])

        def to_p7(r, yy=yy):
            to = (p + r) % 8
            send(recv6.at[yy, to], recv7.at[p, yy], s7, t7, at_p(to))

        each(1, 8, to_p7)
        recv7[p, yy] = recv6[yy, p]
        wide = jnp.concatenate([recv6[yy, b] for b in range(8)], axis=1)
        term = dot(wide, toks[...].reshape(1024, 512)).astype(BF16)
        tall = jnp.concatenate([term[:, q * 128 : q * 128 + 128] for q in range(4)], axis=0)
        send8[pl.ds(yy * 4, 4)] = dot(r8[...], tall).astype(BF16).reshape(4, 48, 128)

        def to_8(r, yy=yy):
            m = yy * 4 + r
            mine = jnp.logical_and(own8, m == own_m)

            @pl.when(mine)
            def _():
                pltpu.make_async_copy(send8.at[m], recv8.at[core * 8 + zl], t8).start()

            @pl.when(jnp.logical_not(mine))
            def _():
                send(send8.at[m], recv8.at[core * 8 + zl], s8, t8, target8(m))

        each(0, 4, to_8)

    take(recv7.at[pl.ds(0, 7)], t7)
    for yy in range(4):
        rows = recv7[:, yy].reshape(384, 128)
        moved = dot(r9[...], rows).astype(BF16)
        for i in range(3):
            for h in range(2):
                gnat[i, (h * 4 + yy) * 64 : (h * 4 + yy) * 64 + 64, :] = moved[i * 128 + h * 64 : i * 128 + h * 64 + 64]
    turned = dot(w[0], gnat[0]) + dot(w[1], gnat[1]) + dot(w[2], gnat[2])
    ig_out[...] = turned.T.astype(BF16)

    take(recv8, t8)
    for c in range(2):
        total = recv8[c * 8].astype(F32)
        for n in range(1, 8):
            total = total + recv8[c * 8 + n].astype(F32)
        total = total * (1.0 / math.sqrt(LENGTH))
        for r in range(4):
            for q in range(4):
                wg_out[r * 2 + c, :, q * 128 : q * 128 + 128] = total[q * 12 + r * 3 : q * 12 + r * 3 + 3]

    take(recv1, s1)
    take(recv2.at[pl.ds(0, 15)], s2)
    take(recv3.at[pl.ds(0, 7)], s3)
    take(recv5.at[pl.ds(0, 15)], s5)
    take(recv6.at[pl.ds(0, 3)], s6)
    take(recv7.at[pl.ds(0, 7)], s7)
    take(toks.at[pl.ds(0, 3)], sx)
    take(toks.at[pl.ds(0, 4)], sc)
    take(recv8.at[pl.ds(0, 15)], s8)

    @pl.when(jnp.logical_not(own8))
    def _():
        take(recv8.at[0], s8)


def on_device(tokens, w_in, grad_out, filters):
    tables = [jnp.asarray(t) for t in selections()] + [jnp.asarray(t) for t in transforms()]
    vmem = pl.BlockSpec(memory_space=pltpu.VMEM)
    dma = pltpu.SemaphoreType.DMA
    input_grad, weight_grad, filter_grad = pl.pallas_call(
        kernel,
        out_shape=(
            jax.ShapeDtypeStruct((128, 512), BF16),
            jax.ShapeDtypeStruct((8, 3, 512), F32),
            jax.ShapeDtypeStruct((64, 128), F32),
        ),
        in_specs=[vmem] * (4 + len(tables)),
        out_specs=(vmem, vmem, vmem),
        scratch_shapes=[
            pltpu.VMEM((4, 384, 128), BF16),
            pltpu.VMEM((3, 384, 128), BF16),
            pltpu.VMEM((16, 32, 128), BF16),
            pltpu.VMEM((16, 32, 128), BF16),
            pltpu.VMEM((8, 32, 128), BF16),
            pltpu.VMEM((8, 32, 128), BF16),
            pltpu.VMEM((8, 32, 128), BF16),
            pltpu.VMEM((16, 32, 128), BF16),
            pltpu.VMEM((4, 8, 48, 128), BF16),
            pltpu.VMEM((8, 4, 48, 128), BF16),
            pltpu.VMEM((16, 48, 128), BF16),
            pltpu.VMEM((16, 48, 128), BF16),
            pltpu.VMEM((8, 128, 512), BF16),
            pltpu.VMEM((3, 512, 128), BF16),
            dma, dma, dma, dma, dma, dma, dma, dma,
            dma, dma((4,)),
            dma, dma, dma, dma, dma, dma, dma, dma,
        ],
        compiler_params=pltpu.CompilerParams(collective_id=0, has_side_effects=True, vmem_limit_bytes=40 * 1024 * 1024),
    )(tokens, w_in.transpose(1, 0, 2), grad_out.T, filters.reshape(64, 128), *tables)
    return input_grad, weight_grad, filter_grad.reshape(1, 1, LENGTH)


def solution(mesh):
    placed = (P("ctx", "tp"), P("tp", None, None), P("ctx", "tp"), P("tp", "ctx", None))
    return jax.shard_map(
        on_device,
        mesh=mesh,
        in_specs=placed,
        out_specs=(P("ctx", "tp"), P("ctx", None, "tp"), P("tp", "ctx", None)),
        check_vma=False,
    )
```

```python
import math

import jax
import jax.numpy as jnp
import numpy as np
from jax import lax
from jax.experimental import pallas as pl
from jax.experimental.pallas import tpu as pltpu
from jax.sharding import PartitionSpec as P

LENGTH = 8192
POINTS = 2 * LENGTH
MESH = pl.DeviceIdType.MESH
F32, BF16 = jnp.float32, jnp.bfloat16
EXACT = lax.Precision.HIGHEST


def selection(outs, ins, pairs):
    matrix = np.zeros((outs, ins), np.float32)
    for row, column in pairs:
        matrix[row, column] = 1.0
    return matrix


def selections():
    def ctx(p, zl):
        return (p >> 1) * 16 + zl * 2 + (p & 1)

    eight = range(8)
    r1 = np.stack([selection(256, 512, [(y * 64 + k, k * 8 + h * 4 + y) for y in range(4) for k in range(64)]) for h in range(2)])
    rg = selection(64, 64, [(y * 16 + h * 8 + n, n * 8 + h * 4 + y) for y in range(4) for h in range(2) for n in eight])
    r2q = selection(256, 192, [(zl * 32 + i * 8 + p, i * 64 + ctx(p, zl)) for zl in eight for i in range(3) for p in eight])
    r2g = np.stack(
        [
            selection(
                256,
                64,
                [
                    (((y % 2) * 4 + n // 2) * 32 + 24 + (own * 2 + y // 2) * 2 + n % 2, y * 16 + h * 8 + n)
                    for y in range(4)
                    for n in eight
                ],
            )
            for own in range(2)
            for h in range(2)
        ]
    )
    r3 = selection(256, 256, [(p * 32 + i * 8 + zl, zl * 32 + i * 8 + p) for zl in eight for i in range(4) for p in eight])
    r5 = selection(192, 192, [(zl * 24 + i * 8 + p, i * 64 + p * 8 + zl) for zl in eight for i in range(3) for p in eight])
    r6 = selection(384, 384, [(p * 48 + z * 3 + i, z * 24 + i * 8 + p) for z in range(16) for i in range(3) for p in eight])
    r8 = selection(
        192,
        192,
        [(zl * 24 + i * 8 + h * 4 + y, y * 48 + h * 24 + zl * 3 + i) for y in range(4) for h in range(2) for zl in eight for i in range(3)],
    )
    r9 = np.stack(
        [
            selection(
                384,
                192,
                [
                    (i * 128 + zl * 16 + c * 8 + h * 4 + y, y * 48 + h * 24 + zl * 3 + i)
                    for y in range(4)
                    for h in range(2)
                    for zl in eight
                    for i in range(3)
                ],
            )
            for c in range(2)
        ]
    )
    return [m.astype(jnp.bfloat16) for m in (r1, rg, r2q, r2g, r3, r5, r6, r8, r9)]


def transforms():
    turn = 2.0 * math.pi
    natural = np.arange(64)
    moved = np.array([(p >> 1) * 16 + zl * 2 + (p & 1) for p in range(8) for zl in range(8)])
    k = np.arange(128)

    def first(rows):
        angle = turn * ((k[:, None] * rows[None, :]) % 128) / 128
        return np.concatenate([np.cos(angle), -np.sin(angle)], 0)

    def last(rows, scale):
        angle = turn * ((rows[:, None] * k[None, :]) % 128) / 128
        return np.concatenate([np.cos(angle), -np.sin(angle)], 1) * scale

    angle = turn * (k[:, None] * k[None, :]) / POINTS
    twist = (np.cos(angle), -np.sin(angle))
    angle = turn * ((k[:, None] * k[None, :]) % 128) / 128
    c, s = np.cos(angle), np.sin(angle)
    forward = np.block([[c, -s], [s, c]])
    back = np.block([[c, s], [-s, c]])
    tables = (
        first(moved),
        first(natural),
        *twist,
        forward,
        back,
        last(moved, 1.0 / POINTS),
        last(natural, 1.0 / (POINTS * math.sqrt(LENGTH))),
    )
    return [t.astype(np.float32) for t in tables]


def dot(left, right, precision=None):
    return jnp.dot(left, right, precision=precision, preferred_element_type=F32)


OPERANDS = [
    "w", "r1", "go", "rg", "r2q", "r2g", "r3", "r5", "r6", "r8", "r9",
    "f1p", "f1n", "twr", "twi", "mf", "mi", "g1p", "g1n",
]


def kernel(tok_in, filt_in, *refs):
    count = len(OPERANDS)
    inputs, refs = refs[:count], refs[count:]
    held, loaded = refs[-count - 1 : -1], refs[-1]
    body(tok_in, filt_in, inputs, held, loaded, *refs[: -count - 1])


def body(
    tok_in, filt_in, inputs, held, loaded,
    ig_out, wg_out, fg_out,
    ig, wg, fg, part, recv1, sendg, recvg, send2, recv2, send3, recv3, send5, recv5, recv6, recv7,
    terms, send8, recv8, toks, turned_w, filt, fg_sent,
    s1, t1, s2, t2, s3, t3, s5, t5, s6, t6, s7, t7, s8, t8, sx, tx, sc, tc, sg, tg, sf, tf, sb, tb, out_sem,
):
    k, j = lax.axis_index("ctx"), lax.axis_index("tp")
    x, zl, core = k // 16, (k // 2) % 8, k % 2
    zh, y = j // 4, j % 4
    z, p = zh * 8 + zl, x * 2 + core

    def at(x_, zl_, core_, zh_, y_):
        return (x_ * 16 + zl_ * 2 + core_, zh_ * 4 + y_)

    def at_y(y_):
        return at(x, zl, core, zh, y_)

    def at_z(z_):
        return at(x, z_ % 8, core, z_ // 8, y)

    def at_p(p_):
        return at(p_ // 2, zl, p_ % 2, zh, y)

    filter_to, filter_from = (j * 8 + k // 8, k % 8), ((k % 8) * 8 + j, k // 8)
    fixed = jnp.logical_and(k == filter_from[0], j == filter_from[1])

    loads = [pltpu.make_async_copy(tok_in, toks.at[p], loaded.at[0])]
    for n, (src, dst) in enumerate(zip(inputs, held)):
        loads.append(pltpu.make_async_copy(src, dst, loaded.at[n + 1]))
    for load in loads[:3]:
        load.start()
    w, r1, go, rg, r2q, r2g, r3, r5, r6, r8, r9, f1p, f1n, twr, twi, mf, mi, g1p, g1n = held
    tok = toks.at[p]

    def need(*names):
        for name in names:
            loads[OPERANDS.index(name) + 1].wait()

    def each(low, high, body):
        def step(n, carry):
            body(n)
            return carry

        lax.fori_loop(low, high, step, 0)

    def send(src, dst, s, t, to):
        pltpu.make_async_remote_copy(
            src_ref=src, dst_ref=dst, send_sem=s, recv_sem=t, device_id=to, device_id_type=MESH
        ).start()

    def take(ref, sem):
        pltpu.make_async_copy(ref, ref, sem).wait()

    owed = {}

    def pay(name):
        owed.pop(name)()

    def finish():
        for name in list(owed):
            pay(name)

    barrier = pltpu.get_barrier_semaphore()

    def greet(to):
        pl.semaphore_signal(barrier, inc=1, device_id=to, device_id_type=MESH)

    each(1, 4, lambda n: greet(at_y((y + n) % 4)))
    each(1, 16, lambda n: greet(at_z((z + n) % 16)))
    each(1, 8, lambda n: greet(at_p((p + n) % 8)))


    @pl.when(jnp.logical_not(fixed))
    def _():
        greet(filter_from)

    for load in loads[3:]:
        load.start()
    loads[0].wait()
    need("w", "r1")

    parts = [dot(tok[...], w[i]).astype(BF16) for i in range(3)]

    def rows_of(h):
        for i in range(3):
            rows = lax.dot_general(r1[h], parts[i], (((1,), (1,)), ((), ())), preferred_element_type=F32).astype(BF16)
            for yy in range(4):
                part[yy, h, i * 64 : i * 64 + 64, :] = rows[yy * 64 : yy * 64 + 64]

    rows_of(1 - zh)
    need("go", "rg")
    sendg[...] = dot(rg[...], go[...]).astype(BF16).reshape(4, 16, 128)
    recvg[y] = sendg[y]

    pl.semaphore_wait(barrier, jnp.where(fixed, 25, 26))
    for n in range(1, 4):
        to = (y + n) % 4
        send(sendg.at[to], recvg.at[y], sg, tg, at_y(to))
    owed["sg"] = lambda: take(recvg.at[pl.ds(0, 3)], sg)
    owed["tg"] = lambda: take(recvg.at[pl.ds(0, 3)], tg)
    for half, h in enumerate((1 - zh, zh)):
        if half == 1:
            rows_of(h)
        for n in range(1, 4):
            to = (y + n) % 4
            send(part.at[to, h], recv1.at[half, n - 1], s1.at[half], t1.at[half], at_y(to))
    for half in range(2):
        owed["t1", half] = lambda half=half: take(recv1.at[half], t1.at[half])
        owed["s1", half] = lambda half=half: take(recv1.at[half], s1.at[half])
    each(1, 4, lambda n: send(tok, toks.at[p], sx, tx, at_p((p + 2 * n) % 8)))
    sibling = x * 2 + (1 - core)
    send(tok, toks.at[p], sc, tc, at_p(sibling))
    owed["tx"] = lambda: take(toks.at[pl.ds(0, 3)], tx)
    owed["sx"] = lambda: take(toks.at[pl.ds(0, 3)], sx)
    owed["tc"] = lambda: take(toks.at[pl.ds(0, 1)], tc)
    owed["sc"] = lambda: take(toks.at[pl.ds(0, 1)], sc)
    def move(src, dst, s, t, to):
        @pl.when(fixed)
        def _():
            pltpu.make_async_copy(src, dst, t).start()

        @pl.when(jnp.logical_not(fixed))
        def _():
            send(src, dst, s, t, to)

    def unless_fixed(ref, sem):
        @pl.when(jnp.logical_not(fixed))
        def _():
            take(ref, sem)

    move(filt_in, filt, sf, tf, filter_to)
    owed["sf"] = lambda: unless_fixed(filt, sf)
    owed["tf"] = lambda: take(filt, tf)
    need(*[name for name in OPERANDS if name not in ("w", "r1", "go", "rg")])

    twist_r, twist_i = twr[...], twi[...]

    def spectrum(table, rows, count):
        a = dot(table[...], rows, EXACT)
        ar, ai = a[:128], a[128:]
        pieces = []
        for n in range(count):
            br, bi = ar[:, n * 128 : n * 128 + 128], ai[:, n * 128 : n * 128 + 128]
            pieces.append(jnp.concatenate([br * twist_r - bi * twist_i, br * twist_i + bi * twist_r], axis=1))
        return dot(jnp.concatenate(pieces, axis=0), mf[...], EXACT)

    def inverse(spectra):
        d = dot(jnp.concatenate(spectra, axis=0), mi[...], EXACT)
        reals, imags = [], []
        for n in range(len(spectra)):
            dr, di = d[n * 128 : n * 128 + 128, :128], d[n * 128 : n * 128 + 128, 128:]
            reals.append(dr * twist_r + di * twist_i)
            imags.append(di * twist_r - dr * twist_i)
        return jnp.concatenate([jnp.concatenate(reals, axis=1), jnp.concatenate(imags, axis=1)], axis=0)

    for b in range(8):
        first = (b // 2) * 128
        wide = jnp.concatenate([w[i, :, first : first + 128] for i in range(3)], axis=1)
        turned_w[b] = dot(wide, r9[b % 2]).astype(BF16)

    def to_z(body):
        def step(n):
            body((z + 8 + (1 - 2 * (n % 2)) * ((n + 1) // 2)) % 16)

        each(0, 15, step)

    def sum_y(half, h):
        pay(("t1", half))
        total = part[y, h].astype(F32)
        for n in range(3):
            total = total + recv1[half, n].astype(F32)
        return total.astype(BF16)

    def slabs(half, h):
        total = sum_y(half, h)
        if half == 0:
            pay("tg")
        cotangent = dot(r2g[zh * 2 + h], recvg[...].reshape(64, 128))
        send2[half] = (dot(r2q[...], total) + cotangent).astype(BF16).reshape(8, 32, 128)

    slabs(0, 1 - zh)

    def to_other(to):
        @pl.when(to // 8 != zh)
        def _():
            send(send2.at[0, to % 8], recv2.at[0, zl], s2.at[0], t2.at[0], at_z(to))

    to_z(to_other)
    owed["t2b"] = lambda: take(recv2.at[0], t2.at[0])
    owed["s2b"] = lambda: take(recv2.at[0], s2.at[0])
    slabs(1, zh)

    def to_own(to):
        @pl.when(to // 8 == zh)
        def _():
            send(send2.at[1, to % 8], recv2.at[1, zl], s2.at[1], t2.at[1], at_z(to))

    to_z(to_own)
    owed["t2a"] = lambda: take(recv2.at[1, pl.ds(0, 7)], t2.at[1])
    owed["s2a"] = lambda: take(recv2.at[1, pl.ds(0, 7)], s2.at[1])
    recv2[1, zl] = send2[1, zl]

    pay("tx")

    def forward(n):
        block = (p + 2 * n) % 8
        send(toks.at[block], toks.at[block], sc, tc, at_p(sibling))

    each(1, 4, forward)
    owed["tc"] = lambda: take(toks.at[pl.ds(0, 4)], tc)
    owed["sc"] = lambda: take(toks.at[pl.ds(0, 4)], sc)

    pay("tf")
    filt_f = spectrum(f1n, filt[...], 1)
    filt_r, filt_i = filt_f[:, :128], filt_f[:, 128:]
    pay("t2a")
    pay("t2b")
    both = recv2[0].astype(F32) + recv2[1].astype(F32)
    moved = dot(r3[...], both.astype(BF16).reshape(256, 128))
    send3[...] = moved.astype(BF16).reshape(8, 32, 128)

    def to_p3(n):
        to = (p + n) % 8
        send(send3.at[to], recv3.at[p], s3, t3, at_p(to))

    each(1, 8, to_p3)
    owed["s3"] = lambda: take(recv3.at[pl.ds(0, 7)], s3)
    owed["t3"] = lambda: take(recv3.at[pl.ds(0, 7)], t3)
    recv3[p] = send3[p]
    pay("t3")

    lines = recv3[...].astype(F32).reshape(8, 4, 8, 128)
    query, key_part, value, cot = [lines[:, i].reshape(64, 128) for i in range(4)]
    spectra = spectrum(f1p, jnp.concatenate([key_part * value, cot * query], axis=1), 2)
    mix_r, mix_i = spectra[:128, :128], spectra[:128, 128:]
    grad_r, grad_i = spectra[128:, :128], spectra[128:, 128:]
    out_f = jnp.concatenate([filt_r * mix_r - filt_i * mix_i, filt_r * mix_i + filt_i * mix_r], axis=1)
    back_f = jnp.concatenate([filt_r * grad_r + filt_i * grad_i, filt_r * grad_i - filt_i * grad_r], axis=1)
    both = dot(g1p[...], inverse([out_f, back_f]), EXACT)
    grad_query = (cot * both[:, :128]).astype(BF16)
    grad_mixed = both[:, 128:].astype(BF16).astype(F32)
    grad_key = (grad_mixed * value).astype(BF16)
    grad_value = (grad_mixed * key_part).astype(BF16)

    rows = jnp.concatenate([grad_query, grad_key, grad_value], axis=0)
    send5[...] = dot(r5[...], rows).reshape(8, 24, 128).astype(BF16)
    to_z(lambda to: send(send5.at[to % 8], recv5.at[z], s5, t5, at_z(to)))
    owed["s5"] = lambda: take(recv5.at[pl.ds(0, 15)], s5)
    owed["t5"] = lambda: take(recv5.at[pl.ds(0, 15)], t5)
    recv5[z] = send5[zl]

    filt_f = jnp.concatenate([mix_r * grad_r + mix_i * grad_i, mix_r * grad_i - mix_i * grad_r], axis=1)
    fg_sent[...] = dot(g1n[...], inverse([filt_f]), EXACT)
    move(fg_sent, fg, sb, tb, filter_from)
    owed["sb"] = lambda: unless_fixed(fg, sb)
    owed["tb"] = lambda: take(fg, tb)
    outs = [pltpu.make_async_copy(src, dst, out_sem.at[n]) for n, (src, dst) in enumerate(((fg, fg_out), (ig, ig_out), (wg, wg_out)))]

    pay("t5")
    moved = dot(r6[...], recv5[...].astype(F32).reshape(384, 128).astype(BF16))
    recv6[y] = moved.astype(BF16).reshape(8, 48, 128)
    for n in range(1, 4):
        send(recv6.at[y], recv6.at[y], s6, t6.at[4 - n], at_y((y + n) % 4))
        owed["t6", n] = lambda n=n: take(recv6.at[(y + n) % 4], t6.at[n])
    owed["s6"] = lambda: take(recv6.at[pl.ds(0, 3)], s6)

    pay("tc")
    for n in (0, 1, 3, 2):
        yy = (y + n) % 4
        if n > 0:
            pay(("t6", n))
        wide = jnp.concatenate([recv6[yy, b] for b in range(8)], axis=1)
        terms[yy] = dot(wide, toks[...].reshape(1024, 512)).astype(BF16)
        if n == 2:
            moved = dot(r8[...], terms[...].reshape(192, 512))
            send8[...] = moved.reshape(8, 24, 512).astype(BF16)

            def to_8(r):
                to = (zl + 4 + (1 - 2 * (r % 2)) * ((r + 1) // 2)) % 8
                send(send8.at[to], recv8.at[zl], s8, t8, at(x, to, core, zh, y))

            each(0, 7, to_8)
            recv8[zl] = send8[zl]

        def to_p7(r, yy=yy):
            to = (p + r) % 8
            send(recv6.at[yy, to], recv7.at[p, yy], s7, t7, at_p(to))

        each(1, 8, to_p7)
        recv7[p, yy] = recv6[yy, p]

    owed["s7"] = lambda: take(recv7.at[pl.ds(0, 7)], s7)
    owed["t7"] = lambda: take(recv7.at[pl.ds(0, 7)], t7)
    owed["s8"] = lambda: take(recv8.at[pl.ds(0, 7)], s8)
    owed["t8"] = lambda: take(recv8.at[pl.ds(0, 7)], t8)
    pay("tb")
    outs[0].start()

    pay("t7")
    total = dot(turned_w[0], recv7[0].reshape(192, 128))
    for b in range(1, 8):
        total = total + dot(turned_w[b], recv7[b].reshape(192, 128))
    ig[...] = total.T.astype(BF16)
    outs[1].start()

    pay("t8")
    total = recv8[0].astype(F32)
    for n in range(1, 8):
        total = total + recv8[n].astype(F32)
    wg[...] = (total * (1.0 / math.sqrt(LENGTH))).reshape(3, 8, 512)
    outs[2].start()

    finish()
    for out in outs:
        out.wait()


def hand_over(*refs):
    sources, results, held, sems = refs[:3], refs[3:6], refs[6:9], refs[9]
    first = [pltpu.make_async_copy(src, dst, sems.at[n]) for n, (src, dst) in enumerate(zip(sources, held))]
    then = [pltpu.make_async_copy(src, dst, sems.at[3 + n]) for n, (src, dst) in enumerate(zip(held, results))]
    for copy in first:
        copy.start()
    for before, copy in zip(first, then):
        before.wait()
        copy.start()
    for copy in then:
        copy.wait()


def on_device(tokens, w_in, grad_out, filters):
    tables = [jnp.asarray(t) for t in selections()] + [jnp.asarray(t) for t in transforms()]
    r1, rg, *rest = tables
    operands = [w_in.transpose(1, 0, 2), r1, grad_out.T, rg, *rest]
    vmem = pl.BlockSpec(memory_space=pltpu.VMEM)
    hbm = pl.BlockSpec(memory_space=pltpu.HBM)
    dma = pltpu.SemaphoreType.DMA
    shapes = (
        jax.ShapeDtypeStruct((128, 512), BF16),
        jax.ShapeDtypeStruct((3, 8, 512), F32),
        jax.ShapeDtypeStruct((64, 128), F32),
    )
    made = pl.pallas_call(
        kernel,
        out_shape=shapes,
        in_specs=[hbm] * (2 + len(operands)),
        out_specs=(hbm, hbm, hbm),
        scratch_shapes=[
            *[pltpu.VMEM(a.shape, a.dtype) for a in shapes],
            pltpu.VMEM((4, 2, 192, 128), BF16),
            pltpu.VMEM((2, 3, 192, 128), BF16),
            pltpu.VMEM((4, 16, 128), BF16),
            pltpu.VMEM((4, 16, 128), BF16),
            pltpu.VMEM((2, 8, 32, 128), BF16),
            pltpu.VMEM((2, 8, 32, 128), BF16),
            pltpu.VMEM((8, 32, 128), BF16),
            pltpu.VMEM((8, 32, 128), BF16),
            pltpu.VMEM((8, 24, 128), BF16),
            pltpu.VMEM((16, 24, 128), BF16),
            pltpu.VMEM((4, 8, 48, 128), BF16),
            pltpu.VMEM((8, 4, 48, 128), BF16),
            pltpu.VMEM((4, 48, 512), BF16),
            pltpu.VMEM((8, 24, 512), BF16),
            pltpu.VMEM((8, 24, 512), BF16),
            pltpu.VMEM((8, 128, 512), BF16),
            pltpu.VMEM((8, 512, 192), BF16),
            pltpu.VMEM((64, 128), F32),
            pltpu.VMEM((64, 128), F32),
            dma((2,)), dma((2,)), dma((2,)), dma((2,)),
            dma, dma, dma, dma,
            dma, dma((4,)),
            dma, dma, dma, dma,
            dma, dma, dma, dma,
            dma, dma, dma, dma, dma, dma,
            dma((3,)),
            *[pltpu.VMEM(a.shape, a.dtype) for a in operands],
            dma((1 + len(operands),)),
        ],
        compiler_params=pltpu.CompilerParams(collective_id=0, has_side_effects=True, vmem_limit_bytes=63 * 1024 * 1024),
    )(tokens, filters.reshape(64, 128), *operands)
    input_grad, weight_grad, filter_grad = pl.pallas_call(
        hand_over,
        out_shape=shapes,
        in_specs=[hbm] * 3,
        out_specs=(hbm, hbm, hbm),
        scratch_shapes=[*[pltpu.VMEM(a.shape, a.dtype) for a in shapes], dma((6,))],
        compiler_params=pltpu.CompilerParams(vmem_limit_bytes=63 * 1024 * 1024),
    )(*made)
    return input_grad, weight_grad.transpose(1, 0, 2), filter_grad.reshape(1, 1, LENGTH)


def solution(mesh):
    placed = (P("ctx", "tp"), P("tp", None, None), P("ctx", "tp"), P("tp", "ctx", None))
    return jax.shard_map(
        on_device,
        mesh=mesh,
        in_specs=placed,
        out_specs=(P("ctx", "tp"), P("ctx", None, "tp"), P("tp", "ctx", None)),
        check_vma=False,
    )
```

```python
import math

import jax
import jax.numpy as jnp
import numpy as np
from jax import lax
from jax.experimental import pallas as pl
from jax.experimental.pallas import tpu as pltpu
from jax.sharding import PartitionSpec as P

LENGTH = 8192
POINTS = 2 * LENGTH
MESH = pl.DeviceIdType.MESH
F32, BF16 = jnp.float32, jnp.bfloat16


def selection(outs, ins, pairs):
    matrix = np.zeros((outs, ins), np.float32)
    for row, column in pairs:
        matrix[row, column] = 1.0
    return matrix


def selections():
    def ctx(p, zl):
        return (p >> 1) * 16 + zl * 2 + (p & 1)

    eight = range(8)
    r1 = np.stack([selection(256, 512, [(y * 64 + k, k * 8 + h * 4 + y) for y in range(4) for k in range(64)]) for h in range(2)])
    rg = selection(64, 64, [(y * 16 + h * 8 + n, n * 8 + h * 4 + y) for y in range(4) for h in range(2) for n in eight])
    r2q = selection(256, 192, [(zl * 32 + i * 8 + p, i * 64 + ctx(p, zl)) for zl in eight for i in range(3) for p in eight])
    r2g = np.stack(
        [
            selection(
                256,
                64,
                [
                    (((y % 2) * 4 + n // 2) * 32 + 24 + (own * 2 + y // 2) * 2 + n % 2, y * 16 + h * 8 + n)
                    for y in range(4)
                    for n in eight
                ],
            )
            for own in range(2)
            for h in range(2)
        ]
    )
    r3 = selection(256, 256, [(p * 32 + i * 8 + zl, zl * 32 + i * 8 + p) for zl in eight for i in range(4) for p in eight])
    r5 = selection(192, 192, [(zl * 24 + i * 8 + p, i * 64 + p * 8 + zl) for zl in eight for i in range(3) for p in eight])
    r6 = selection(384, 384, [(p * 48 + z * 3 + i, z * 24 + i * 8 + p) for z in range(16) for i in range(3) for p in eight])
    r8 = selection(
        192,
        192,
        [(zl * 24 + q * 6 + h * 3 + i, q * 48 + h * 24 + zl * 3 + i) for q in range(4) for h in range(2) for zl in eight for i in range(3)],
    )
    r9 = np.stack(
        [
            selection(
                384,
                192,
                [
                    (i * 128 + zl * 16 + c * 8 + h * 4 + y, y * 48 + h * 24 + zl * 3 + i)
                    for y in range(4)
                    for h in range(2)
                    for zl in eight
                    for i in range(3)
                ],
            )
            for c in range(2)
        ]
    )
    return [m.astype(jnp.bfloat16) for m in (r1, rg, r2q, r2g, r3, r5, r6, r8, r9)]


def transforms():
    turn = 2.0 * math.pi
    natural = np.arange(64)
    moved = np.array([(p >> 1) * 16 + zl * 2 + (p & 1) for p in range(8) for zl in range(8)])
    k = np.arange(128)

    def first(rows):
        angle = turn * ((k[:, None] * rows[None, :]) % 128) / 128
        return np.concatenate([np.cos(angle), -np.sin(angle)], 0)

    def last(rows, scale):
        angle = turn * ((rows[:, None] * k[None, :]) % 128) / 128
        return np.concatenate([np.cos(angle), -np.sin(angle)], 1) * scale

    angle = turn * (k[:, None] * k[None, :]) / POINTS
    twist = (np.cos(angle), -np.sin(angle))
    angle = turn * ((k[:, None] * k[None, :]) % 128) / 128
    c, s = np.cos(angle), np.sin(angle)
    forward = np.block([[c, -s], [s, c]])
    back = np.block([[c, s], [-s, c]])
    tables = (
        first(moved),
        first(natural),
        *twist,
        forward,
        back,
        last(moved, 1.0 / POINTS),
        last(natural, 1.0 / (POINTS * math.sqrt(LENGTH))),
    )
    axes = (1, 1, None, None, 0, 0, 1, 1)
    return [t.astype(np.float32) if a is None else pieces_of_table(t, a) for t, a in zip(tables, axes)]


def pieces_of_table(table, axis):
    high = table.astype(jnp.bfloat16)
    low = (table - high.astype(np.float64)).astype(jnp.bfloat16)
    return np.concatenate([high, high, low], axis=axis)


def pieces_of(values, axis):
    high = values.astype(BF16)
    low = (values - high.astype(F32)).astype(BF16)
    return jnp.concatenate([high, low, high], axis=axis)


def dot(left, right):
    return jnp.dot(left, right, preferred_element_type=F32)


OPERANDS = [
    "w", "r1", "go", "rg", "r2q", "r2g", "r3", "r5", "r6", "r8", "r9",
    "f1p", "f1n", "twr", "twi", "mf", "mi", "g1p", "g1n",
]


def kernel(tok_in, filt_in, *refs):
    count = len(OPERANDS)
    inputs, refs = refs[:count], refs[count:]
    held, loaded = refs[-count - 1 : -1], refs[-1]
    body(tok_in, filt_in, inputs, held, loaded, *refs[: -count - 1])


def body(
    tok_in, filt_in, inputs, held, loaded,
    ig_out, wg_out, fg_out,
    ig, wg, fg, part, recv1, sendg, recvg, send2, recv2, send3, recv3, send5, recv5, recv6, recv7,
    send8, recv8, toks, turned_w, filt, fg_sent,
    s1, t1, s2, t2, s3, t3, s5, t5, s6, t6, s7, t7, s8, t8, sx, tx, sc, tc, sg, tg, sf, tf, sb, tb, out_sem,
):
    k, j = lax.axis_index("ctx"), lax.axis_index("tp")
    x, zl, core = k // 16, (k // 2) % 8, k % 2
    zh, y = j // 4, j % 4
    z, p = zh * 8 + zl, x * 2 + core

    def at(x_, zl_, core_, zh_, y_):
        return (x_ * 16 + zl_ * 2 + core_, zh_ * 4 + y_)

    def at_y(y_):
        return at(x, zl, core, zh, y_)

    def at_z(z_):
        return at(x, z_ % 8, core, z_ // 8, y)

    def at_p(p_):
        return at(p_ // 2, zl, p_ % 2, zh, y)

    filter_to, filter_from = (j * 8 + k // 8, k % 8), ((k % 8) * 8 + j, k // 8)
    fixed = jnp.logical_and(k == filter_from[0], j == filter_from[1])

    loads = [pltpu.make_async_copy(tok_in, toks.at[p], loaded.at[0])]
    for n, (src, dst) in enumerate(zip(inputs, held)):
        loads.append(pltpu.make_async_copy(src, dst, loaded.at[n + 1]))
    for load in loads[:3]:
        load.start()
    w, r1, go, rg, r2q, r2g, r3, r5, r6, r8, r9, f1p, f1n, twr, twi, mf, mi, g1p, g1n = held
    tok = toks.at[p]

    def need(*names):
        for name in names:
            loads[OPERANDS.index(name) + 1].wait()

    def each(low, high, body):
        def step(n, carry):
            body(n)
            return carry

        lax.fori_loop(low, high, step, 0)

    def send(src, dst, s, t, to):
        pltpu.make_async_remote_copy(
            src_ref=src, dst_ref=dst, send_sem=s, recv_sem=t, device_id=to, device_id_type=MESH
        ).start()

    def take(ref, sem):
        pltpu.make_async_copy(ref, ref, sem).wait()

    owed = {}

    def pay(name):
        owed.pop(name)()

    def finish():
        for name in list(owed):
            pay(name)

    barrier = pltpu.get_barrier_semaphore()

    def greet(to):
        pl.semaphore_signal(barrier, inc=1, device_id=to, device_id_type=MESH)

    each(1, 4, lambda n: greet(at_y((y + n) % 4)))
    each(1, 16, lambda n: greet(at_z((z + n) % 16)))
    each(1, 8, lambda n: greet(at_p((p + n) % 8)))


    @pl.when(jnp.logical_not(fixed))
    def _():
        greet(filter_from)

    for load in loads[3:]:
        load.start()
    loads[0].wait()
    need("w", "r1")

    parts = [dot(tok[...], w[i]).astype(BF16) for i in range(3)]

    def rows_of(h):
        for i in range(3):
            rows = lax.dot_general(r1[h], parts[i], (((1,), (1,)), ((), ())), preferred_element_type=F32).astype(BF16)
            for yy in range(4):
                part[yy, h, i * 64 : i * 64 + 64, :] = rows[yy * 64 : yy * 64 + 64]

    rows_of(1 - zh)
    need("go", "rg")
    sendg[...] = dot(rg[...], go[...]).astype(BF16).reshape(4, 16, 128)
    recvg[y] = sendg[y]

    pl.semaphore_wait(barrier, jnp.where(fixed, 25, 26))
    for n in range(1, 4):
        to = (y + n) % 4
        send(sendg.at[to], recvg.at[y], sg, tg, at_y(to))
    owed["sg"] = lambda: take(recvg.at[pl.ds(0, 3)], sg)
    owed["tg"] = lambda: take(recvg.at[pl.ds(0, 3)], tg)
    for half, h in enumerate((1 - zh, zh)):
        if half == 1:
            rows_of(h)
        for n in range(1, 4):
            to = (y + n) % 4
            send(part.at[to, h], recv1.at[half, n - 1], s1.at[half], t1.at[half], at_y(to))
    for half in range(2):
        owed["t1", half] = lambda half=half: take(recv1.at[half], t1.at[half])
        owed["s1", half] = lambda half=half: take(recv1.at[half], s1.at[half])
    each(1, 4, lambda n: send(tok, toks.at[p], sx, tx, at_p((p + 2 * n) % 8)))
    sibling = x * 2 + (1 - core)
    send(tok, toks.at[p], sc, tc, at_p(sibling))
    owed["tx"] = lambda: take(toks.at[pl.ds(0, 3)], tx)
    owed["sx"] = lambda: take(toks.at[pl.ds(0, 3)], sx)
    owed["tc"] = lambda: take(toks.at[pl.ds(0, 1)], tc)
    owed["sc"] = lambda: take(toks.at[pl.ds(0, 1)], sc)
    def move(src, dst, s, t, to):
        @pl.when(fixed)
        def _():
            pltpu.make_async_copy(src, dst, t).start()

        @pl.when(jnp.logical_not(fixed))
        def _():
            send(src, dst, s, t, to)

    def unless_fixed(ref, sem):
        @pl.when(jnp.logical_not(fixed))
        def _():
            take(ref, sem)

    move(filt_in, filt, sf, tf, filter_to)
    owed["sf"] = lambda: unless_fixed(filt, sf)
    owed["tf"] = lambda: take(filt, tf)
    need(*[name for name in OPERANDS if name not in ("w", "r1", "go", "rg")])

    twist_r, twist_i = twr[...], twi[...]

    def spectrum(table, rows, count):
        a = dot(table[...], pieces_of(rows, 0))
        ar, ai = a[:128], a[128:]
        pieces = []
        for n in range(count):
            br, bi = ar[:, n * 128 : n * 128 + 128], ai[:, n * 128 : n * 128 + 128]
            pieces.append(jnp.concatenate([br * twist_r - bi * twist_i, br * twist_i + bi * twist_r], axis=1))
        return dot(pieces_of(jnp.concatenate(pieces, axis=0), 1), mf[...])

    def inverse(spectra):
        d = dot(pieces_of(jnp.concatenate(spectra, axis=0), 1), mi[...])
        reals, imags = [], []
        for n in range(len(spectra)):
            dr, di = d[n * 128 : n * 128 + 128, :128], d[n * 128 : n * 128 + 128, 128:]
            reals.append(dr * twist_r + di * twist_i)
            imags.append(di * twist_r - dr * twist_i)
        return jnp.concatenate([jnp.concatenate(reals, axis=1), jnp.concatenate(imags, axis=1)], axis=0)

    def to_z(body):
        def step(n):
            body((z + 8 + (1 - 2 * (n % 2)) * ((n + 1) // 2)) % 16)

        each(0, 15, step)

    def sum_y(half, h):
        pay(("t1", half))
        total = part[y, h].astype(F32)
        for n in range(3):
            total = total + recv1[half, n].astype(F32)
        return total.astype(BF16)

    def slabs(half, h):
        total = sum_y(half, h)
        if half == 0:
            pay("tg")
        cotangent = dot(r2g[zh * 2 + h], recvg[...].reshape(64, 128))
        send2[half] = (dot(r2q[...], total) + cotangent).astype(BF16).reshape(8, 32, 128)

    slabs(0, 1 - zh)

    def to_other(to):
        @pl.when(to // 8 != zh)
        def _():
            send(send2.at[0, to % 8], recv2.at[0, zl], s2.at[0], t2.at[0], at_z(to))

    to_z(to_other)
    owed["t2b"] = lambda: take(recv2.at[0], t2.at[0])
    owed["s2b"] = lambda: take(recv2.at[0], s2.at[0])
    slabs(1, zh)

    def to_own(to):
        @pl.when(to // 8 == zh)
        def _():
            send(send2.at[1, to % 8], recv2.at[1, zl], s2.at[1], t2.at[1], at_z(to))

    to_z(to_own)
    owed["t2a"] = lambda: take(recv2.at[1, pl.ds(0, 7)], t2.at[1])
    owed["s2a"] = lambda: take(recv2.at[1, pl.ds(0, 7)], s2.at[1])
    recv2[1, zl] = send2[1, zl]

    pay("t2a")
    pay("t2b")
    both = recv2[0].astype(F32) + recv2[1].astype(F32)
    moved = dot(r3[...], both.astype(BF16).reshape(256, 128))
    send3[...] = moved.astype(BF16).reshape(8, 32, 128)

    def to_p3(n):
        to = (p + n) % 8
        send(send3.at[to], recv3.at[p], s3, t3, at_p(to))

    each(1, 8, to_p3)
    owed["s3"] = lambda: take(recv3.at[pl.ds(0, 7)], s3)
    owed["t3"] = lambda: take(recv3.at[pl.ds(0, 7)], t3)
    recv3[p] = send3[p]
    pay("tx")

    def forward(n):
        block = (p + 2 * n) % 8
        send(toks.at[block], toks.at[block], sc, tc, at_p(sibling))

    each(1, 4, forward)
    owed["tc"] = lambda: take(toks.at[pl.ds(0, 4)], tc)
    owed["sc"] = lambda: take(toks.at[pl.ds(0, 4)], sc)

    pay("tf")
    filt_f = spectrum(f1n, filt[...], 1)
    filt_r, filt_i = filt_f[:, :128], filt_f[:, 128:]
    pay("t3")

    lines = recv3[...].astype(F32).reshape(8, 4, 8, 128)
    query, key_part, value, cot = [lines[:, i].reshape(64, 128) for i in range(4)]
    spectra = spectrum(f1p, jnp.concatenate([key_part * value, cot * query], axis=1), 2)
    mix_r, mix_i = spectra[:128, :128], spectra[:128, 128:]
    grad_r, grad_i = spectra[128:, :128], spectra[128:, 128:]
    out_f = jnp.concatenate([filt_r * mix_r - filt_i * mix_i, filt_r * mix_i + filt_i * mix_r], axis=1)
    back_f = jnp.concatenate([filt_r * grad_r + filt_i * grad_i, filt_r * grad_i - filt_i * grad_r], axis=1)
    both = dot(g1p[...], pieces_of(inverse([out_f, back_f]), 0))
    grad_query = (cot * both[:, :128]).astype(BF16)
    grad_mixed = both[:, 128:].astype(BF16).astype(F32)
    grad_key = (grad_mixed * value).astype(BF16)
    grad_value = (grad_mixed * key_part).astype(BF16)

    rows = jnp.concatenate([grad_query, grad_key, grad_value], axis=0)
    send5[...] = dot(r5[...], rows).reshape(8, 24, 128).astype(BF16)
    to_z(lambda to: send(send5.at[to % 8], recv5.at[z], s5, t5, at_z(to)))
    owed["s5"] = lambda: take(recv5.at[pl.ds(0, 15)], s5)
    owed["t5"] = lambda: take(recv5.at[pl.ds(0, 15)], t5)
    recv5[z] = send5[zl]

    filt_f = jnp.concatenate([mix_r * grad_r + mix_i * grad_i, mix_r * grad_i - mix_i * grad_r], axis=1)
    fg_sent[...] = dot(g1n[...], pieces_of(inverse([filt_f]), 0))
    move(fg_sent, fg, sb, tb, filter_from)
    owed["sb"] = lambda: unless_fixed(fg, sb)
    owed["tb"] = lambda: take(fg, tb)
    outs = [pltpu.make_async_copy(src, dst, out_sem.at[n]) for n, (src, dst) in enumerate(((fg, fg_out), (ig, ig_out), (wg, wg_out)))]

    for b in range(8):
        first = (b // 2) * 128
        wide = jnp.concatenate([w[i, :, first : first + 128] for i in range(3)], axis=1)
        turned_w[b] = dot(wide, r9[b % 2]).astype(BF16)

    pay("t5")
    moved = dot(r6[...], recv5[...].astype(F32).reshape(384, 128).astype(BF16))
    recv6[y] = moved.astype(BF16).reshape(8, 48, 128)
    for n in (1, 3, 2):
        send(recv6.at[y], recv6.at[y], s6, t6.at[4 - n], at_y((y + n) % 4))
        owed["t6", n] = lambda n=n: take(recv6.at[(y + n) % 4], t6.at[n])
    owed["s6"] = lambda: take(recv6.at[pl.ds(0, 3)], s6)

    def far_first_8(body):
        def step(n):
            to = zl + (1 - 2 * (n % 2)) * (7 - n // 2)

            @pl.when(jnp.logical_and(to >= 0, to < 8))
            def _():
                body(to)

        each(0, 14, step)

    def weight_terms(those):
        wide = [jnp.concatenate([recv6[yy, b] for b in range(8)], axis=1) for yy in those]
        term = dot(jnp.concatenate(wide, axis=0), toks[...].reshape(1024, 512)).astype(BF16)
        for n, yy in enumerate(those):
            tall = jnp.concatenate([term[n * 48 : n * 48 + 48, q * 128 : q * 128 + 128] for q in range(4)], axis=0)
            send8[yy] = dot(r8[...], tall).reshape(8, 24, 128).astype(BF16)
            far_first_8(lambda to, yy=yy: send(send8.at[yy, to], recv8.at[zl, yy], s8, t8, at(x, to, core, zh, y)))
            recv8[zl, yy] = send8[yy, zl]

    def to_owners(yy):
        def to_p7(r):
            to = (p + r) % 8
            send(recv6.at[yy, to], recv7.at[p, yy], s7, t7, at_p(to))

        each(1, 8, to_p7)
        recv7[p, yy] = recv6[yy, p]

    pay("tc")
    weight_terms([y])
    to_owners(y)
    pay(("t6", 1))
    pay(("t6", 3))
    weight_terms([(y + 1) % 4, (y + 3) % 4])
    pay(("t6", 2))
    weight_terms([(y + 2) % 4])
    for n in (1, 3, 2):
        to_owners((y + n) % 4)

    owed["s7"] = lambda: take(recv7.at[pl.ds(0, 7)], s7)
    owed["t7"] = lambda: take(recv7.at[pl.ds(0, 7)], t7)
    owed["s8"] = lambda: take(recv8.at[pl.ds(0, 7)], s8)
    owed["t8"] = lambda: take(recv8.at[pl.ds(0, 7)], t8)
    pay("tb")
    outs[0].start()

    pay("t7")
    total = dot(turned_w[0], recv7[0].reshape(192, 128))
    for b in range(1, 8):
        total = total + dot(turned_w[b], recv7[b].reshape(192, 128))
    ig[...] = total.T.astype(BF16)
    outs[1].start()

    pay("t8")
    total = recv8[0].astype(F32)
    for n in range(1, 8):
        total = total + recv8[n].astype(F32)
    total = total * (1.0 / math.sqrt(LENGTH))
    for yy in range(4):
        for q in range(4):
            for h in range(2):
                for i in range(3):
                    row = q * 6 + h * 3 + i
                    wg[i, h * 4 + yy : h * 4 + yy + 1, q * 128 : q * 128 + 128] = total[yy, row : row + 1]
    outs[2].start()

    finish()
    for out in outs:
        out.wait()


def hand_over(*refs):
    sources, results, held, sems = refs[:3], refs[3:6], refs[6:9], refs[9]
    first = [pltpu.make_async_copy(src, dst, sems.at[n]) for n, (src, dst) in enumerate(zip(sources, held))]
    then = [pltpu.make_async_copy(src, dst, sems.at[3 + n]) for n, (src, dst) in enumerate(zip(held, results))]
    for copy in first:
        copy.start()
    for before, copy in zip(first, then):
        before.wait()
        copy.start()
    for copy in then:
        copy.wait()


def on_device(tokens, w_in, grad_out, filters):
    tables = [jnp.asarray(t) for t in selections()] + [jnp.asarray(t) for t in transforms()]
    r1, rg, *rest = tables
    operands = [w_in.transpose(1, 0, 2), r1, grad_out.T, rg, *rest]
    vmem = pl.BlockSpec(memory_space=pltpu.VMEM)
    hbm = pl.BlockSpec(memory_space=pltpu.HBM)
    dma = pltpu.SemaphoreType.DMA
    shapes = (
        jax.ShapeDtypeStruct((128, 512), BF16),
        jax.ShapeDtypeStruct((3, 8, 512), F32),
        jax.ShapeDtypeStruct((64, 128), F32),
    )
    made = pl.pallas_call(
        kernel,
        out_shape=shapes,
        in_specs=[hbm] * (2 + len(operands)),
        out_specs=(hbm, hbm, hbm),
        scratch_shapes=[
            *[pltpu.VMEM(a.shape, a.dtype) for a in shapes],
            pltpu.VMEM((4, 2, 192, 128), BF16),
            pltpu.VMEM((2, 3, 192, 128), BF16),
            pltpu.VMEM((4, 16, 128), BF16),
            pltpu.VMEM((4, 16, 128), BF16),
            pltpu.VMEM((2, 8, 32, 128), BF16),
            pltpu.VMEM((2, 8, 32, 128), BF16),
            pltpu.VMEM((8, 32, 128), BF16),
            pltpu.VMEM((8, 32, 128), BF16),
            pltpu.VMEM((8, 24, 128), BF16),
            pltpu.VMEM((16, 24, 128), BF16),
            pltpu.VMEM((4, 8, 48, 128), BF16),
            pltpu.VMEM((8, 4, 48, 128), BF16),
            pltpu.VMEM((4, 8, 24, 128), BF16),
            pltpu.VMEM((8, 4, 24, 128), BF16),
            pltpu.VMEM((8, 128, 512), BF16),
            pltpu.VMEM((8, 512, 192), BF16),
            pltpu.VMEM((64, 128), F32),
            pltpu.VMEM((64, 128), F32),
            dma((2,)), dma((2,)), dma((2,)), dma((2,)),
            dma, dma, dma, dma,
            dma, dma((4,)),
            dma, dma, dma, dma,
            dma, dma, dma, dma,
            dma, dma, dma, dma, dma, dma,
            dma((3,)),
            *[pltpu.VMEM(a.shape, a.dtype) for a in operands],
            dma((1 + len(operands),)),
        ],
        compiler_params=pltpu.CompilerParams(collective_id=0, has_side_effects=True, vmem_limit_bytes=63 * 1024 * 1024),
    )(tokens, filters.reshape(64, 128), *operands)
    input_grad, weight_grad, filter_grad = pl.pallas_call(
        hand_over,
        out_shape=shapes,
        in_specs=[hbm] * 3,
        out_specs=(hbm, hbm, hbm),
        scratch_shapes=[*[pltpu.VMEM(a.shape, a.dtype) for a in shapes], dma((6,))],
        compiler_params=pltpu.CompilerParams(vmem_limit_bytes=63 * 1024 * 1024),
    )(*made)
    return input_grad, weight_grad.transpose(1, 0, 2), filter_grad.reshape(1, 1, LENGTH)


def solution(mesh):
    placed = (P("ctx", "tp"), P("tp", None, None), P("ctx", "tp"), P("tp", "ctx", None))
    return jax.shard_map(
        on_device,
        mesh=mesh,
        in_specs=placed,
        out_specs=(P("ctx", "tp"), P("ctx", None, "tp"), P("tp", "ctx", None)),
        check_vma=False,
    )
```

```python
import math

import jax
import jax.numpy as jnp
import numpy as np
from jax import lax
from jax.experimental import pallas as pl
from jax.experimental.pallas import tpu as pltpu
from jax.sharding import PartitionSpec as P

LENGTH = 8192
POINTS = 2 * LENGTH
MESH = pl.DeviceIdType.MESH
F32, BF16 = jnp.float32, jnp.bfloat16


def selection(outs, ins, pairs):
    matrix = np.zeros((outs, ins), np.float32)
    for row, column in pairs:
        matrix[row, column] = 1.0
    return matrix


def selections():
    def ctx(p, zl):
        return (p >> 1) * 16 + zl * 2 + (p & 1)

    eight = range(8)
    r1 = np.stack([selection(256, 512, [(y * 64 + k, k * 8 + h * 4 + y) for y in range(4) for k in range(64)]) for h in range(2)])
    rg = selection(64, 64, [(y * 16 + h * 8 + n, n * 8 + h * 4 + y) for y in range(4) for h in range(2) for n in eight])
    r2q = selection(256, 192, [(zl * 32 + i * 8 + p, i * 64 + ctx(p, zl)) for zl in eight for i in range(3) for p in eight])
    r2g = np.stack(
        [
            selection(
                256,
                64,
                [
                    (((y % 2) * 4 + n // 2) * 32 + 24 + (own * 2 + y // 2) * 2 + n % 2, y * 16 + h * 8 + n)
                    for y in range(4)
                    for n in eight
                ],
            )
            for own in range(2)
            for h in range(2)
        ]
    )
    r3 = selection(256, 256, [(p * 32 + i * 8 + zl, zl * 32 + i * 8 + p) for zl in eight for i in range(4) for p in eight])
    r5 = selection(192, 192, [(zl * 24 + i * 8 + p, i * 64 + p * 8 + zl) for zl in eight for i in range(3) for p in eight])
    r6 = selection(384, 384, [(p * 48 + z * 3 + i, z * 24 + i * 8 + p) for z in range(16) for i in range(3) for p in eight])
    r8 = selection(
        192,
        192,
        [(zl * 24 + q * 6 + h * 3 + i, q * 48 + h * 24 + zl * 3 + i) for q in range(4) for h in range(2) for zl in eight for i in range(3)],
    )
    r9 = np.concatenate(
        [
            selection(
                384,
                192,
                [
                    (i * 128 + zl * 16 + c * 8 + h * 4 + y, y * 48 + h * 24 + zl * 3 + i)
                    for y in range(4)
                    for h in range(2)
                    for zl in eight
                    for i in range(3)
                ],
            )
            for c in range(2)
        ],
        axis=1,
    )
    return [m.astype(jnp.bfloat16) for m in (r1, rg, r2q, r2g, r3, r5, r6, r8, r9)]


def transforms():
    turn = 2.0 * math.pi
    natural = np.arange(64)
    moved = np.array([(p >> 1) * 16 + zl * 2 + (p & 1) for p in range(8) for zl in range(8)])
    k = np.arange(128)

    def first(rows):
        angle = turn * ((k[:, None] * rows[None, :]) % 128) / 128
        return np.concatenate([np.cos(angle), -np.sin(angle)], 0)

    def last(rows, scale):
        angle = turn * ((rows[:, None] * k[None, :]) % 128) / 128
        return np.concatenate([np.cos(angle), -np.sin(angle)], 1) * scale

    angle = turn * (k[:, None] * k[None, :]) / POINTS
    twist = (np.cos(angle), -np.sin(angle))
    angle = turn * ((k[:, None] * k[None, :]) % 128) / 128
    c, s = np.cos(angle), np.sin(angle)
    forward = np.block([[c, -s], [s, c]])
    back = np.block([[c, s], [-s, c]])
    tables = (
        first(moved),
        first(natural),
        *twist,
        forward,
        back,
        last(moved, 1.0 / POINTS),
        last(natural, 1.0 / (POINTS * math.sqrt(LENGTH))),
    )
    axes = (1, 1, None, None, 0, 0, 1, 1)
    return [t.astype(np.float32) if a is None else pieces_of_table(t, a) for t, a in zip(tables, axes)]


def pieces_of_table(table, axis):
    high = table.astype(jnp.bfloat16)
    low = (table - high.astype(np.float64)).astype(jnp.bfloat16)
    return np.concatenate([high, high, low], axis=axis)


def pieces_of(values, axis):
    high = values.astype(BF16)
    low = (values - high.astype(F32)).astype(BF16)
    return jnp.concatenate([high, low, high], axis=axis)


def dot(left, right):
    return jnp.dot(left, right, preferred_element_type=F32)


OPERANDS = [
    "w", "r1", "go", "rg", "r2q", "r2g", "r3", "r5", "r6", "r8", "r9",
    "f1p", "f1n", "twr", "twi", "mf", "mi", "g1p", "g1n",
]


def kernel(tok_in, filt_in, *refs):
    count = len(OPERANDS)
    inputs, refs = refs[:count], refs[count:]
    held, loaded = refs[-count - 1 : -1], refs[-1]
    body(tok_in, filt_in, inputs, held, loaded, *refs[: -count - 1])


def body(
    tok_in, filt_in, inputs, held, loaded,
    ig_out, wg_out, fg_out,
    ig, wg, fg, part, recv1, sendg, recvg, send2, recv2, send3, recv3, send5, recv5, recv6, recv7,
    send8, recv8, toks, turned_w, filt, fg_sent,
    s1, t1, s2, t2, s3, t3, s5, t5, s6, t6, s7, t7, s8, t8, sx, tx, sc, tc, sg, tg, sf, tf, sb, tb, out_sem,
):
    k, j = lax.axis_index("ctx"), lax.axis_index("tp")
    x, zl, core = k // 16, (k // 2) % 8, k % 2
    zh, y = j // 4, j % 4
    z, p = zh * 8 + zl, x * 2 + core

    def at(x_, zl_, core_, zh_, y_):
        return (x_ * 16 + zl_ * 2 + core_, zh_ * 4 + y_)

    def at_y(y_):
        return at(x, zl, core, zh, y_)

    def at_z(z_):
        return at(x, z_ % 8, core, z_ // 8, y)

    def at_p(p_):
        return at(p_ // 2, zl, p_ % 2, zh, y)

    filter_to, filter_from = (j * 8 + k // 8, k % 8), ((k % 8) * 8 + j, k // 8)
    fixed = jnp.logical_and(k == filter_from[0], j == filter_from[1])

    loads = [pltpu.make_async_copy(tok_in, toks.at[p], loaded.at[0])]
    for n, (src, dst) in enumerate(zip(inputs, held)):
        loads.append(pltpu.make_async_copy(src, dst, loaded.at[n + 1]))
    for load in loads[:3]:
        load.start()
    w, r1, go, rg, r2q, r2g, r3, r5, r6, r8, r9, f1p, f1n, twr, twi, mf, mi, g1p, g1n = held
    tok = toks.at[p]

    def need(*names):
        for name in names:
            loads[OPERANDS.index(name) + 1].wait()

    def each(low, high, body):
        def step(n, carry):
            body(n)
            return carry

        lax.fori_loop(low, high, step, 0)

    def send(src, dst, s, t, to):
        pltpu.make_async_remote_copy(
            src_ref=src, dst_ref=dst, send_sem=s, recv_sem=t, device_id=to, device_id_type=MESH
        ).start()

    def take(ref, sem):
        pltpu.make_async_copy(ref, ref, sem).wait()

    owed = {}

    def pay(name):
        owed.pop(name)()

    def finish():
        for name in list(owed):
            pay(name)

    barrier = pltpu.get_barrier_semaphore()

    def greet(to):
        pl.semaphore_signal(barrier, inc=1, device_id=to, device_id_type=MESH)

    def far_first_16(body):
        def step(n):
            body((z + 8 + (1 - 2 * (n % 2)) * ((n + 1) // 2)) % 16)

        each(0, 15, step)

    each(1, 4, lambda n: greet(at_y((y + n) % 4)))
    @pl.when(jnp.logical_not(fixed))
    def _():
        greet(filter_from)

    each(1, 16, lambda n: greet(at_z((z + n) % 16)))
    each(1, 8, lambda n: greet(at_p((p + n) % 8)))
    for load in loads[3:]:
        load.start()
    loads[0].wait()
    need("w", "r1")

    parts = [dot(tok[...], w[i]).astype(BF16) for i in range(3)]

    def rows_of(h):
        for i in range(3):
            rows = lax.dot_general(r1[h], parts[i], (((1,), (1,)), ((), ())), preferred_element_type=F32).astype(BF16)
            for yy in range(4):
                part[yy, h, i * 64 : i * 64 + 64, :] = rows[yy * 64 : yy * 64 + 64]

    rows_of(1 - zh)
    need("go", "rg")
    sendg[...] = dot(rg[...], go[...]).astype(BF16).reshape(4, 16, 128)
    recvg[y] = sendg[y]

    pl.semaphore_wait(barrier, jnp.where(fixed, 25, 26))
    for n in range(1, 4):
        to = (y + n) % 4
        send(sendg.at[to], recvg.at[y], sg, tg, at_y(to))
    owed["sg"] = lambda: take(recvg.at[pl.ds(0, 3)], sg)
    owed["tg"] = lambda: take(recvg.at[pl.ds(0, 3)], tg)
    for half, h in enumerate((1 - zh, zh)):
        if half == 1:
            rows_of(h)
        for n in range(1, 4):
            to = (y + n) % 4
            send(part.at[to, h], recv1.at[half, n - 1], s1.at[half], t1.at[half], at_y(to))
    for half in range(2):
        owed["t1", half] = lambda half=half: take(recv1.at[half], t1.at[half])
        owed["s1", half] = lambda half=half: take(recv1.at[half], s1.at[half])
    each(1, 4, lambda n: send(tok, toks.at[p], sx, tx, at_p((p + 2 * n) % 8)))
    sibling = x * 2 + (1 - core)
    send(tok, toks.at[p], sc, tc, at_p(sibling))
    owed["tx"] = lambda: take(toks.at[pl.ds(0, 3)], tx)
    owed["sx"] = lambda: take(toks.at[pl.ds(0, 3)], sx)
    owed["tc"] = lambda: take(toks.at[pl.ds(0, 1)], tc)
    owed["sc"] = lambda: take(toks.at[pl.ds(0, 1)], sc)
    def move(src, dst, s, t, to):
        @pl.when(fixed)
        def _():
            pltpu.make_async_copy(src, dst, t).start()

        @pl.when(jnp.logical_not(fixed))
        def _():
            send(src, dst, s, t, to)

    def unless_fixed(ref, sem):
        @pl.when(jnp.logical_not(fixed))
        def _():
            take(ref, sem)

    move(filt_in, filt, sf, tf, filter_to)
    owed["sf"] = lambda: unless_fixed(filt, sf)
    owed["tf"] = lambda: take(filt, tf)
    need(*[name for name in OPERANDS if name not in ("w", "r1", "go", "rg")])

    twist_r, twist_i = twr[...], twi[...]

    def spectrum(table, rows, count):
        a = dot(table[...], pieces_of(rows, 0))
        ar, ai = a[:128], a[128:]
        pieces = []
        for n in range(count):
            br, bi = ar[:, n * 128 : n * 128 + 128], ai[:, n * 128 : n * 128 + 128]
            pieces.append(jnp.concatenate([br * twist_r - bi * twist_i, br * twist_i + bi * twist_r], axis=1))
        return dot(pieces_of(jnp.concatenate(pieces, axis=0), 1), mf[...])

    def inverse(spectra):
        d = dot(pieces_of(jnp.concatenate(spectra, axis=0), 1), mi[...])
        reals, imags = [], []
        for n in range(len(spectra)):
            dr, di = d[n * 128 : n * 128 + 128, :128], d[n * 128 : n * 128 + 128, 128:]
            reals.append(dr * twist_r + di * twist_i)
            imags.append(di * twist_r - dr * twist_i)
        return jnp.concatenate([jnp.concatenate(reals, axis=1), jnp.concatenate(imags, axis=1)], axis=0)

    def sum_y(half, h):
        pay(("t1", half))
        total = part[y, h].astype(F32)
        for n in range(3):
            total = total + recv1[half, n].astype(F32)
        return total.astype(BF16)

    def slabs(half, h):
        total = sum_y(half, h)
        if half == 0:
            pay("tg")
        cotangent = dot(r2g[zh * 2 + h], recvg[...].reshape(64, 128))
        send2[half] = (dot(r2q[...], total) + cotangent).astype(BF16).reshape(8, 32, 128)

    slabs(0, 1 - zh)

    def to_other(to):
        @pl.when(to // 8 != zh)
        def _():
            send(send2.at[0, to % 8], recv2.at[0, zl], s2.at[0], t2.at[0], at_z(to))

    far_first_16(to_other)
    owed["t2b"] = lambda: take(recv2.at[0], t2.at[0])
    owed["s2b"] = lambda: take(recv2.at[0], s2.at[0])
    slabs(1, zh)

    def to_own(to):
        @pl.when(to // 8 == zh)
        def _():
            send(send2.at[1, to % 8], recv2.at[1, zl], s2.at[1], t2.at[1], at_z(to))

    far_first_16(to_own)
    owed["t2a"] = lambda: take(recv2.at[1, pl.ds(0, 7)], t2.at[1])
    owed["s2a"] = lambda: take(recv2.at[1, pl.ds(0, 7)], s2.at[1])
    recv2[1, zl] = send2[1, zl]

    pay("t2a")
    pay("t2b")
    both = recv2[0].astype(F32) + recv2[1].astype(F32)
    moved = dot(r3[...], both.astype(BF16).reshape(256, 128))
    send3[...] = moved.astype(BF16).reshape(8, 32, 128)

    def to_p3(n):
        to = (p + n) % 8
        send(send3.at[to], recv3.at[p], s3, t3, at_p(to))

    each(1, 8, to_p3)
    owed["s3"] = lambda: take(recv3.at[pl.ds(0, 7)], s3)
    owed["t3"] = lambda: take(recv3.at[pl.ds(0, 7)], t3)
    recv3[p] = send3[p]
    pay("tx")

    def forward(n):
        block = (p + 2 * n) % 8
        send(toks.at[block], toks.at[block], sc, tc, at_p(sibling))

    each(1, 4, forward)
    owed["tc"] = lambda: take(toks.at[pl.ds(0, 4)], tc)
    owed["sc"] = lambda: take(toks.at[pl.ds(0, 4)], sc)

    pay("tf")
    filt_f = spectrum(f1n, filt[...], 1)
    filt_r, filt_i = filt_f[:, :128], filt_f[:, 128:]
    pay("t3")

    lines = recv3[...].astype(F32).reshape(8, 4, 8, 128)
    query, key_part, value, cot = [lines[:, i].reshape(64, 128) for i in range(4)]
    spectra = spectrum(f1p, jnp.concatenate([key_part * value, cot * query], axis=1), 2)
    mix_r, mix_i = spectra[:128, :128], spectra[:128, 128:]
    grad_r, grad_i = spectra[128:, :128], spectra[128:, 128:]
    out_f = jnp.concatenate([filt_r * mix_r - filt_i * mix_i, filt_r * mix_i + filt_i * mix_r], axis=1)
    back_f = jnp.concatenate([filt_r * grad_r + filt_i * grad_i, filt_r * grad_i - filt_i * grad_r], axis=1)
    both = dot(g1p[...], pieces_of(inverse([out_f, back_f]), 0))
    grad_query = (cot * both[:, :128]).astype(BF16)
    grad_mixed = both[:, 128:].astype(BF16).astype(F32)
    grad_key = (grad_mixed * value).astype(BF16)
    grad_value = (grad_mixed * key_part).astype(BF16)

    rows = jnp.concatenate([grad_query, grad_key, grad_value], axis=0)
    send5[...] = dot(r5[...], rows).reshape(8, 24, 128).astype(BF16)
    far_first_16(lambda to: send(send5.at[to % 8], recv5.at[z], s5, t5, at_z(to)))
    owed["s5"] = lambda: take(recv5.at[pl.ds(0, 15)], s5)
    owed["t5"] = lambda: take(recv5.at[pl.ds(0, 15)], t5)
    recv5[z] = send5[zl]

    filt_f = jnp.concatenate([mix_r * grad_r + mix_i * grad_i, mix_r * grad_i - mix_i * grad_r], axis=1)
    fg_sent[...] = dot(g1n[...], pieces_of(inverse([filt_f]), 0))
    move(fg_sent, fg, sb, tb, filter_from)
    owed["sb"] = lambda: unless_fixed(fg, sb)
    owed["tb"] = lambda: take(fg, tb)
    outs = [pltpu.make_async_copy(src, dst, out_sem.at[n]) for n, (src, dst) in enumerate(((fg, fg_out), (ig, ig_out), (wg, wg_out)))]

    for b in range(4):
        wide = jnp.concatenate([w[i, :, b * 128 : b * 128 + 128] for i in range(3)], axis=1)
        turned_w[:, b * 384 : b * 384 + 384] = dot(wide, r9[...]).astype(BF16)

    pay("t5")
    moved = dot(r6[...], recv5[...].astype(F32).reshape(384, 128).astype(BF16))
    recv6[y] = moved.astype(BF16).reshape(8, 48, 128)
    for n in (1, 3, 2):
        send(recv6.at[y], recv6.at[y], s6, t6.at[4 - n], at_y((y + n) % 4))
        owed["t6", n] = lambda n=n: take(recv6.at[(y + n) % 4], t6.at[n])
    owed["s6"] = lambda: take(recv6.at[pl.ds(0, 3)], s6)

    def far_first_8(body):
        def step(n):
            to = zl + (1 - 2 * (n % 2)) * (7 - n // 2)

            @pl.when(jnp.logical_and(to >= 0, to < 8))
            def _():
                body(to)

        each(0, 14, step)

    def weight_terms(those):
        wide = [jnp.concatenate([recv6[yy, b] for b in range(8)], axis=1) for yy in those]
        term = dot(jnp.concatenate(wide, axis=0), toks[...].reshape(1024, 512)).astype(BF16)
        for n, yy in enumerate(those):
            tall = jnp.concatenate([term[n * 48 : n * 48 + 48, q * 128 : q * 128 + 128] for q in range(4)], axis=0)
            send8[yy] = dot(r8[...], tall).reshape(8, 24, 128).astype(BF16)
            far_first_8(lambda to, yy=yy: send(send8.at[yy, to], recv8.at[zl, yy], s8, t8, at(x, to, core, zh, y)))
            recv8[zl, yy] = send8[yy, zl]

    def to_owners(yy):
        def to_p7(r):
            to = (p + r) % 8
            send(recv6.at[yy, to], recv7.at[p, yy], s7, t7, at_p(to))

        each(1, 8, to_p7)
        recv7[p, yy] = recv6[yy, p]

    pay("tc")
    weight_terms([y])
    to_owners(y)
    pay(("t6", 1))
    pay(("t6", 3))
    weight_terms([(y + 1) % 4, (y + 3) % 4])
    to_owners((y + 1) % 4)
    to_owners((y + 3) % 4)
    pay(("t6", 2))
    weight_terms([(y + 2) % 4])
    to_owners((y + 2) % 4)

    owed["s7"] = lambda: take(recv7.at[pl.ds(0, 7)], s7)
    owed["t7"] = lambda: take(recv7.at[pl.ds(0, 7)], t7)
    owed["s8"] = lambda: take(recv8.at[pl.ds(0, 7)], s8)
    owed["t8"] = lambda: take(recv8.at[pl.ds(0, 7)], t8)
    pay("tb")
    outs[0].start()

    pay("t7")
    total = dot(turned_w[...], recv7[...].reshape(1536, 128))
    ig[...] = total.T.astype(BF16)
    outs[1].start()

    pay("t8")
    total = recv8[0].astype(F32)
    for n in range(1, 8):
        total = total + recv8[n].astype(F32)
    total = total * (1.0 / math.sqrt(LENGTH))
    for yy in range(4):
        for q in range(4):
            for h in range(2):
                for i in range(3):
                    row = q * 6 + h * 3 + i
                    wg[i, h * 4 + yy : h * 4 + yy + 1, q * 128 : q * 128 + 128] = total[yy, row : row + 1]
    outs[2].start()

    finish()
    for out in outs:
        out.wait()


def hand_over(*refs):
    sources, results, held, sems = refs[:3], refs[3:6], refs[6:9], refs[9]
    first = [pltpu.make_async_copy(src, dst, sems.at[n]) for n, (src, dst) in enumerate(zip(sources, held))]
    then = [pltpu.make_async_copy(src, dst, sems.at[3 + n]) for n, (src, dst) in enumerate(zip(held, results))]
    for copy in first:
        copy.start()
    for before, copy in zip(first, then):
        before.wait()
        copy.start()
    for copy in then:
        copy.wait()


def on_device(tokens, w_in, grad_out, filters):
    tables = [jnp.asarray(t) for t in selections()] + [jnp.asarray(t) for t in transforms()]
    r1, rg, *rest = tables
    operands = [w_in.transpose(1, 0, 2), r1, grad_out.T, rg, *rest]
    vmem = pl.BlockSpec(memory_space=pltpu.VMEM)
    hbm = pl.BlockSpec(memory_space=pltpu.HBM)
    dma = pltpu.SemaphoreType.DMA
    shapes = (
        jax.ShapeDtypeStruct((128, 512), BF16),
        jax.ShapeDtypeStruct((3, 8, 512), F32),
        jax.ShapeDtypeStruct((64, 128), F32),
    )
    made = pl.pallas_call(
        kernel,
        out_shape=shapes,
        in_specs=[hbm] * (2 + len(operands)),
        out_specs=(hbm, hbm, hbm),
        scratch_shapes=[
            *[pltpu.VMEM(a.shape, a.dtype) for a in shapes],
            pltpu.VMEM((4, 2, 192, 128), BF16),
            pltpu.VMEM((2, 3, 192, 128), BF16),
            pltpu.VMEM((4, 16, 128), BF16),
            pltpu.VMEM((4, 16, 128), BF16),
            pltpu.VMEM((2, 8, 32, 128), BF16),
            pltpu.VMEM((2, 8, 32, 128), BF16),
            pltpu.VMEM((8, 32, 128), BF16),
            pltpu.VMEM((8, 32, 128), BF16),
            pltpu.VMEM((8, 24, 128), BF16),
            pltpu.VMEM((16, 24, 128), BF16),
            pltpu.VMEM((4, 8, 48, 128), BF16),
            pltpu.VMEM((8, 4, 48, 128), BF16),
            pltpu.VMEM((4, 8, 24, 128), BF16),
            pltpu.VMEM((8, 4, 24, 128), BF16),
            pltpu.VMEM((8, 128, 512), BF16),
            pltpu.VMEM((512, 1536), BF16),
            pltpu.VMEM((64, 128), F32),
            pltpu.VMEM((64, 128), F32),
            dma((2,)), dma((2,)), dma((2,)), dma((2,)),
            dma, dma, dma, dma,
            dma, dma((4,)),
            dma, dma, dma, dma,
            dma, dma, dma, dma,
            dma, dma, dma, dma, dma, dma,
            dma((3,)),
            *[pltpu.VMEM(a.shape, a.dtype) for a in operands],
            dma((1 + len(operands),)),
        ],
        compiler_params=pltpu.CompilerParams(collective_id=0, has_side_effects=True, vmem_limit_bytes=63 * 1024 * 1024),
    )(tokens, filters.reshape(64, 128), *operands)
    input_grad, weight_grad, filter_grad = pl.pallas_call(
        hand_over,
        out_shape=shapes,
        in_specs=[hbm] * 3,
        out_specs=(hbm, hbm, hbm),
        scratch_shapes=[*[pltpu.VMEM(a.shape, a.dtype) for a in shapes], dma((6,))],
        compiler_params=pltpu.CompilerParams(vmem_limit_bytes=63 * 1024 * 1024),
    )(*made)
    return input_grad, weight_grad.transpose(1, 0, 2), filter_grad.reshape(1, 1, LENGTH)


def solution(mesh):
    placed = (P("ctx", "tp"), P("tp", None, None), P("ctx", "tp"), P("tp", "ctx", None))
    return jax.shard_map(
        on_device,
        mesh=mesh,
        in_specs=placed,
        out_specs=(P("ctx", "tp"), P("ctx", None, "tp"), P("tp", "ctx", None)),
        check_vma=False,
    )
```

```python
import math

import jax
import jax.numpy as jnp
import numpy as np
from jax import lax
from jax.experimental import pallas as pl
from jax.experimental.pallas import tpu as pltpu
from jax.sharding import PartitionSpec as P

LENGTH = 8192
POINTS = 2 * LENGTH
MESH = pl.DeviceIdType.MESH
F32, BF16 = jnp.float32, jnp.bfloat16


def selection(outs, ins, pairs):
    matrix = np.zeros((outs, ins), np.float32)
    for row, column in pairs:
        matrix[row, column] = 1.0
    return matrix


def selections():
    def ctx(p, zl):
        return (p >> 1) * 16 + zl * 2 + (p & 1)

    eight = range(8)
    r1 = np.stack([selection(256, 512, [(y * 64 + k, k * 8 + h * 4 + y) for y in range(4) for k in range(64)]) for h in range(2)])
    rg = selection(64, 64, [(y * 16 + h * 8 + n, n * 8 + h * 4 + y) for y in range(4) for h in range(2) for n in eight])
    r2q = selection(256, 192, [(zl * 32 + i * 8 + p, i * 64 + ctx(p, zl)) for zl in eight for i in range(3) for p in eight])
    r2g = np.stack(
        [
            selection(
                256,
                64,
                [
                    (((y % 2) * 4 + n // 2) * 32 + 24 + (own * 2 + y // 2) * 2 + n % 2, y * 16 + h * 8 + n)
                    for y in range(4)
                    for n in eight
                ],
            )
            for own in range(2)
            for h in range(2)
        ]
    )
    r3 = selection(256, 256, [(p * 32 + i * 8 + zl, zl * 32 + i * 8 + p) for zl in eight for i in range(4) for p in eight])
    r5 = selection(192, 192, [(zl * 24 + i * 8 + p, i * 64 + p * 8 + zl) for zl in eight for i in range(3) for p in eight])
    r6 = selection(384, 384, [(p * 48 + z * 3 + i, z * 24 + i * 8 + p) for z in range(16) for i in range(3) for p in eight])
    r8 = selection(
        192,
        192,
        [(zl * 24 + q * 6 + h * 3 + i, q * 48 + h * 24 + zl * 3 + i) for q in range(4) for h in range(2) for zl in eight for i in range(3)],
    )
    r9 = np.stack(
        [
            selection(
                384,
                192,
                [
                    (i * 128 + zl * 16 + c * 8 + h * 4 + y, y * 48 + h * 24 + zl * 3 + i)
                    for y in range(4)
                    for h in range(2)
                    for zl in eight
                    for i in range(3)
                ],
            )
            for c in range(2)
        ]
    )
    return [m.astype(jnp.bfloat16) for m in (r1, rg, r2q, r2g, r3, r5, r6, r8, r9)]


def transforms():
    turn = 2.0 * math.pi
    natural = np.arange(64)
    moved = np.array([(p >> 1) * 16 + zl * 2 + (p & 1) for p in range(8) for zl in range(8)])
    k = np.arange(128)

    def first(rows):
        angle = turn * ((k[:, None] * rows[None, :]) % 128) / 128
        return np.concatenate([np.cos(angle), -np.sin(angle)], 0)

    def last(rows, scale):
        angle = turn * ((rows[:, None] * k[None, :]) % 128) / 128
        return np.concatenate([np.cos(angle), -np.sin(angle)], 1) * scale

    angle = turn * (k[:, None] * k[None, :]) / POINTS
    twist = (np.cos(angle), -np.sin(angle))
    angle = turn * ((k[:, None] * k[None, :]) % 128) / 128
    c, s = np.cos(angle), np.sin(angle)
    forward = np.block([[c, -s], [s, c]])
    back = np.block([[c, s], [-s, c]])
    tables = (
        first(moved),
        first(natural),
        *twist,
        forward,
        back,
        last(moved, 1.0 / POINTS),
        last(natural, 1.0 / (POINTS * math.sqrt(LENGTH))),
    )
    axes = (1, 1, None, None, 0, 0, 1, 1)
    return [t.astype(np.float32) if a is None else pieces_of_table(t, a) for t, a in zip(tables, axes)]


def pieces_of_table(table, axis):
    high = table.astype(jnp.bfloat16)
    low = (table - high.astype(np.float64)).astype(jnp.bfloat16)
    return np.concatenate([high, high, low], axis=axis)


def pieces_of(values, axis):
    high = values.astype(BF16)
    low = (values - high.astype(F32)).astype(BF16)
    return jnp.concatenate([high, low, high], axis=axis)


def dot(left, right):
    return jnp.dot(left, right, preferred_element_type=F32)


OPERANDS = [
    "w", "r1", "go", "rg", "r2q", "r2g", "r3", "r5", "r6", "r8", "r9",
    "f1p", "f1n", "twr", "twi", "mf", "mi", "g1p", "g1n",
]


def kernel(tok_in, filt_in, *refs):
    count = len(OPERANDS)
    inputs, refs = refs[:count], refs[count:]
    held, loaded = refs[-count - 1 : -1], refs[-1]
    body(tok_in, filt_in, inputs, held, loaded, *refs[: -count - 1])


def body(
    tok_in, filt_in, inputs, held, loaded,
    ig_out, wg_out, fg_out,
    ig, wg, fg, part, recv1, sendg, recvg, send2, recv2, send3, recv3, send5, recv5, recv6, recv7,
    send8, recv8, toks, turned_w, filt, fg_sent,
    s1, t1, s2, t2, s3, t3, s5, t5, s6, t6, s7, t7, s8, t8, sx, tx, sc, tc, sg, tg, sf, tf, sb, tb, out_sem,
):
    k, j = lax.axis_index("ctx"), lax.axis_index("tp")
    x, zl, core = k // 16, (k // 2) % 8, k % 2
    zh, y = j // 4, j % 4
    z, p = zh * 8 + zl, x * 2 + core

    def at(x_, zl_, core_, zh_, y_):
        return (x_ * 16 + zl_ * 2 + core_, zh_ * 4 + y_)

    def at_y(y_):
        return at(x, zl, core, zh, y_)

    def at_z(z_):
        return at(x, z_ % 8, core, z_ // 8, y)

    def at_p(p_):
        return at(p_ // 2, zl, p_ % 2, zh, y)

    filter_to, filter_from = (j * 8 + k // 8, k % 8), ((k % 8) * 8 + j, k // 8)
    fixed = jnp.logical_and(k == filter_from[0], j == filter_from[1])

    loads = [pltpu.make_async_copy(tok_in, toks.at[p], loaded.at[0])]
    for n, (src, dst) in enumerate(zip(inputs, held)):
        loads.append(pltpu.make_async_copy(src, dst, loaded.at[n + 1]))
    for load in loads[:3]:
        load.start()
    w, r1, go, rg, r2q, r2g, r3, r5, r6, r8, r9, f1p, f1n, twr, twi, mf, mi, g1p, g1n = held
    tok = toks.at[p]

    def need(*names):
        for name in names:
            loads[OPERANDS.index(name) + 1].wait()

    def each(low, high, body):
        def step(n, carry):
            body(n)
            return carry

        lax.fori_loop(low, high, step, 0)

    def send(src, dst, s, t, to):
        pltpu.make_async_remote_copy(
            src_ref=src, dst_ref=dst, send_sem=s, recv_sem=t, device_id=to, device_id_type=MESH
        ).start()

    def take(ref, sem):
        pltpu.make_async_copy(ref, ref, sem).wait()

    owed = {}

    def pay(name):
        owed.pop(name)()

    def finish():
        for name in list(owed):
            pay(name)

    barrier = pltpu.get_barrier_semaphore()

    def greet(to):
        pl.semaphore_signal(barrier, inc=1, device_id=to, device_id_type=MESH)

    each(1, 4, lambda n: greet(at_y((y + n) % 4)))
    each(1, 16, lambda n: greet(at_z((z + n) % 16)))
    each(1, 8, lambda n: greet(at_p((p + n) % 8)))


    @pl.when(jnp.logical_not(fixed))
    def _():
        greet(filter_from)

    for load in loads[3:]:
        load.start()
    loads[0].wait()
    need("w", "r1")

    parts = [dot(tok[...], w[i]).astype(BF16) for i in range(3)]

    def rows_of(h):
        for i in range(3):
            rows = lax.dot_general(r1[h], parts[i], (((1,), (1,)), ((), ())), preferred_element_type=F32).astype(BF16)
            for yy in range(4):
                part[yy, h, i * 64 : i * 64 + 64, :] = rows[yy * 64 : yy * 64 + 64]

    rows_of(1 - zh)
    need("go", "rg")
    sendg[...] = dot(rg[...], go[...]).astype(BF16).reshape(4, 16, 128)
    recvg[y] = sendg[y]

    pl.semaphore_wait(barrier, jnp.where(fixed, 25, 26))
    for n in range(1, 4):
        to = (y + n) % 4
        send(sendg.at[to], recvg.at[y], sg, tg, at_y(to))
    owed["sg"] = lambda: take(recvg.at[pl.ds(0, 3)], sg)
    owed["tg"] = lambda: take(recvg.at[pl.ds(0, 3)], tg)
    for half, h in enumerate((1 - zh, zh)):
        if half == 1:
            rows_of(h)
        for n in range(1, 4):
            to = (y + n) % 4
            send(part.at[to, h], recv1.at[half, n - 1], s1.at[half], t1.at[half], at_y(to))
    for half in range(2):
        owed["t1", half] = lambda half=half: take(recv1.at[half], t1.at[half])
        owed["s1", half] = lambda half=half: take(recv1.at[half], s1.at[half])
    each(1, 4, lambda n: send(tok, toks.at[p], sx, tx, at_p((p + 2 * n) % 8)))
    sibling = x * 2 + (1 - core)
    send(tok, toks.at[p], sc, tc, at_p(sibling))
    owed["tx"] = lambda: take(toks.at[pl.ds(0, 3)], tx)
    owed["sx"] = lambda: take(toks.at[pl.ds(0, 3)], sx)
    owed["tc"] = lambda: take(toks.at[pl.ds(0, 1)], tc)
    owed["sc"] = lambda: take(toks.at[pl.ds(0, 1)], sc)
    def move(src, dst, s, t, to):
        @pl.when(fixed)
        def _():
            pltpu.make_async_copy(src, dst, t).start()

        @pl.when(jnp.logical_not(fixed))
        def _():
            send(src, dst, s, t, to)

    def unless_fixed(ref, sem):
        @pl.when(jnp.logical_not(fixed))
        def _():
            take(ref, sem)

    move(filt_in, filt, sf, tf, filter_to)
    owed["sf"] = lambda: unless_fixed(filt, sf)
    owed["tf"] = lambda: take(filt, tf)
    need(*[name for name in OPERANDS if name not in ("w", "r1", "go", "rg")])

    twist_r, twist_i = twr[...], twi[...]

    def spectrum(table, rows, count):
        a = dot(table[...], pieces_of(rows, 0))
        ar, ai = a[:128], a[128:]
        pieces = []
        for n in range(count):
            br, bi = ar[:, n * 128 : n * 128 + 128], ai[:, n * 128 : n * 128 + 128]
            pieces.append(jnp.concatenate([br * twist_r - bi * twist_i, br * twist_i + bi * twist_r], axis=1))
        return dot(pieces_of(jnp.concatenate(pieces, axis=0), 1), mf[...])

    def inverse(spectra):
        d = dot(pieces_of(jnp.concatenate(spectra, axis=0), 1), mi[...])
        reals, imags = [], []
        for n in range(len(spectra)):
            dr, di = d[n * 128 : n * 128 + 128, :128], d[n * 128 : n * 128 + 128, 128:]
            reals.append(dr * twist_r + di * twist_i)
            imags.append(di * twist_r - dr * twist_i)
        return jnp.concatenate([jnp.concatenate(reals, axis=1), jnp.concatenate(imags, axis=1)], axis=0)

    def to_z(body):
        def step(n):
            body((z + 8 + (1 - 2 * (n % 2)) * ((n + 1) // 2)) % 16)

        each(0, 15, step)

    def sum_y(half, h):
        pay(("t1", half))
        total = part[y, h].astype(F32)
        for n in range(3):
            total = total + recv1[half, n].astype(F32)
        return total.astype(BF16)

    def slabs(half, h):
        total = sum_y(half, h)
        if half == 0:
            pay("tg")
        cotangent = dot(r2g[zh * 2 + h], recvg[...].reshape(64, 128))
        send2[half] = (dot(r2q[...], total) + cotangent).astype(BF16).reshape(8, 32, 128)

    slabs(0, 1 - zh)

    def to_other(to):
        @pl.when(to // 8 != zh)
        def _():
            send(send2.at[0, to % 8], recv2.at[0, zl], s2.at[0], t2.at[0], at_z(to))

    to_z(to_other)
    owed["t2b"] = lambda: take(recv2.at[0], t2.at[0])
    owed["s2b"] = lambda: take(recv2.at[0], s2.at[0])
    slabs(1, zh)

    def to_own(to):
        @pl.when(to // 8 == zh)
        def _():
            send(send2.at[1, to % 8], recv2.at[1, zl], s2.at[1], t2.at[1], at_z(to))

    to_z(to_own)
    owed["t2a"] = lambda: take(recv2.at[1, pl.ds(0, 7)], t2.at[1])
    owed["s2a"] = lambda: take(recv2.at[1, pl.ds(0, 7)], s2.at[1])
    recv2[1, zl] = send2[1, zl]

    pay("t2a")
    pay("t2b")
    both = recv2[0].astype(F32) + recv2[1].astype(F32)
    moved = dot(r3[...], both.astype(BF16).reshape(256, 128))
    send3[...] = moved.astype(BF16).reshape(8, 32, 128)

    def to_p3(n):
        to = (p + n) % 8
        send(send3.at[to], recv3.at[p], s3, t3, at_p(to))

    each(1, 8, to_p3)
    owed["s3"] = lambda: take(recv3.at[pl.ds(0, 7)], s3)
    owed["t3"] = lambda: take(recv3.at[pl.ds(0, 7)], t3)
    recv3[p] = send3[p]
    pay("tx")

    def forward(n):
        block = (p + 2 * n) % 8
        send(toks.at[block], toks.at[block], sc, tc, at_p(sibling))

    each(1, 4, forward)
    owed["tc"] = lambda: take(toks.at[pl.ds(0, 4)], tc)
    owed["sc"] = lambda: take(toks.at[pl.ds(0, 4)], sc)

    pay("tf")
    filt_f = spectrum(f1n, filt[...], 1)
    filt_r, filt_i = filt_f[:, :128], filt_f[:, 128:]
    pay("t3")

    lines = recv3[...].astype(F32).reshape(8, 4, 8, 128)
    query, key_part, value, cot = [lines[:, i].reshape(64, 128) for i in range(4)]
    spectra = spectrum(f1p, jnp.concatenate([key_part * value, cot * query], axis=1), 2)
    mix_r, mix_i = spectra[:128, :128], spectra[:128, 128:]
    grad_r, grad_i = spectra[128:, :128], spectra[128:, 128:]
    out_f = jnp.concatenate([filt_r * mix_r - filt_i * mix_i, filt_r * mix_i + filt_i * mix_r], axis=1)
    back_f = jnp.concatenate([filt_r * grad_r + filt_i * grad_i, filt_r * grad_i - filt_i * grad_r], axis=1)
    both = dot(g1p[...], pieces_of(inverse([out_f, back_f]), 0))
    grad_query = (cot * both[:, :128]).astype(BF16)
    grad_mixed = both[:, 128:].astype(BF16).astype(F32)
    grad_key = (grad_mixed * value).astype(BF16)
    grad_value = (grad_mixed * key_part).astype(BF16)

    rows = jnp.concatenate([grad_query, grad_key, grad_value], axis=0)
    send5[...] = dot(r5[...], rows).reshape(8, 24, 128).astype(BF16)
    to_z(lambda to: send(send5.at[to % 8], recv5.at[z], s5, t5, at_z(to)))
    owed["s5"] = lambda: take(recv5.at[pl.ds(0, 15)], s5)
    owed["t5"] = lambda: take(recv5.at[pl.ds(0, 15)], t5)
    recv5[z] = send5[zl]

    filt_f = jnp.concatenate([mix_r * grad_r + mix_i * grad_i, mix_r * grad_i - mix_i * grad_r], axis=1)
    fg_sent[...] = dot(g1n[...], pieces_of(inverse([filt_f]), 0))
    move(fg_sent, fg, sb, tb, filter_from)
    owed["sb"] = lambda: unless_fixed(fg, sb)
    owed["tb"] = lambda: take(fg, tb)
    outs = [pltpu.make_async_copy(src, dst, out_sem.at[n]) for n, (src, dst) in enumerate(((fg, fg_out), (ig, ig_out), (wg, wg_out)))]

    for b in range(8):
        first = (b // 2) * 128
        wide = jnp.concatenate([w[i, :, first : first + 128] for i in range(3)], axis=1)
        turned_w[b] = dot(wide, r9[b % 2]).astype(BF16)

    pay("t5")
    moved = dot(r6[...], recv5[...].astype(F32).reshape(384, 128).astype(BF16))
    recv6[y] = moved.astype(BF16).reshape(8, 48, 128)
    for n in (1, 3, 2):
        send(recv6.at[y], recv6.at[y], s6, t6.at[4 - n], at_y((y + n) % 4))
        owed["t6", n] = lambda n=n: take(recv6.at[(y + n) % 4], t6.at[n])
    owed["s6"] = lambda: take(recv6.at[pl.ds(0, 3)], s6)

    def far_first_8(body):
        def step(n):
            to = zl + (1 - 2 * (n % 2)) * (7 - n // 2)

            @pl.when(jnp.logical_and(to >= 0, to < 8))
            def _():
                body(to)

        each(0, 14, step)

    def weight_terms(those):
        wide = [jnp.concatenate([recv6[yy, b] for b in range(8)], axis=1) for yy in those]
        term = dot(jnp.concatenate(wide, axis=0), toks[...].reshape(1024, 512)).astype(BF16)
        for n, yy in enumerate(those):
            tall = jnp.concatenate([term[n * 48 : n * 48 + 48, q * 128 : q * 128 + 128] for q in range(4)], axis=0)
            send8[yy] = dot(r8[...], tall).reshape(8, 24, 128).astype(BF16)
            far_first_8(lambda to, yy=yy: send(send8.at[yy, to], recv8.at[zl, yy], s8, t8, at(x, to, core, zh, y)))
            recv8[zl, yy] = send8[yy, zl]

    def to_owners(yy):
        def to_p7(r):
            to = (p + r) % 8
            send(recv6.at[yy, to], recv7.at[p, yy], s7, t7, at_p(to))

        each(1, 8, to_p7)
        recv7[p, yy] = recv6[yy, p]

    pay("tc")
    weight_terms([y])
    to_owners(y)
    pay(("t6", 1))
    pay(("t6", 3))
    weight_terms([(y + 1) % 4, (y + 3) % 4])
    pay(("t6", 2))
    weight_terms([(y + 2) % 4])
    for n in (1, 3, 2):
        to_owners((y + n) % 4)

    owed["s7"] = lambda: take(recv7.at[pl.ds(0, 7)], s7)
    owed["t7"] = lambda: take(recv7.at[pl.ds(0, 7)], t7)
    owed["s8"] = lambda: take(recv8.at[pl.ds(0, 7)], s8)
    owed["t8"] = lambda: take(recv8.at[pl.ds(0, 7)], t8)

    pay("t7")
    total = dot(turned_w[0], recv7[0].reshape(192, 128))
    for b in range(1, 8):
        total = total + dot(turned_w[b], recv7[b].reshape(192, 128))
    ig[...] = total.T.astype(BF16)
    outs[1].start()
    pay("tb")
    outs[0].start()

    pay("t8")
    total = recv8[0].astype(F32)
    for n in range(1, 8):
        total = total + recv8[n].astype(F32)
    total = total * (1.0 / math.sqrt(LENGTH))
    for yy in range(4):
        for q in range(4):
            for h in range(2):
                for i in range(3):
                    row = q * 6 + h * 3 + i
                    wg[i, h * 4 + yy : h * 4 + yy + 1, q * 128 : q * 128 + 128] = total[yy, row : row + 1]
    outs[2].start()

    finish()
    for out in outs:
        out.wait()


def hand_over(*refs):
    sources, results, held, sems = refs[:3], refs[3:6], refs[6:9], refs[9]
    first = [pltpu.make_async_copy(src, dst, sems.at[n]) for n, (src, dst) in enumerate(zip(sources, held))]
    then = [pltpu.make_async_copy(src, dst, sems.at[3 + n]) for n, (src, dst) in enumerate(zip(held, results))]
    for copy in first:
        copy.start()
    for before, copy in zip(first, then):
        before.wait()
        copy.start()
    for copy in then:
        copy.wait()


def on_device(tokens, w_in, grad_out, filters):
    tables = [jnp.asarray(t) for t in selections()] + [jnp.asarray(t) for t in transforms()]
    r1, rg, *rest = tables
    operands = [w_in.transpose(1, 0, 2), r1, grad_out.T, rg, *rest]
    vmem = pl.BlockSpec(memory_space=pltpu.VMEM)
    hbm = pl.BlockSpec(memory_space=pltpu.HBM)
    dma = pltpu.SemaphoreType.DMA
    shapes = (
        jax.ShapeDtypeStruct((128, 512), BF16),
        jax.ShapeDtypeStruct((3, 8, 512), F32),
        jax.ShapeDtypeStruct((64, 128), F32),
    )
    made = pl.pallas_call(
        kernel,
        out_shape=shapes,
        in_specs=[hbm] * (2 + len(operands)),
        out_specs=(hbm, hbm, hbm),
        scratch_shapes=[
            *[pltpu.VMEM(a.shape, a.dtype) for a in shapes],
            pltpu.VMEM((4, 2, 192, 128), BF16),
            pltpu.VMEM((2, 3, 192, 128), BF16),
            pltpu.VMEM((4, 16, 128), BF16),
            pltpu.VMEM((4, 16, 128), BF16),
            pltpu.VMEM((2, 8, 32, 128), BF16),
            pltpu.VMEM((2, 8, 32, 128), BF16),
            pltpu.VMEM((8, 32, 128), BF16),
            pltpu.VMEM((8, 32, 128), BF16),
            pltpu.VMEM((8, 24, 128), BF16),
            pltpu.VMEM((16, 24, 128), BF16),
            pltpu.VMEM((4, 8, 48, 128), BF16),
            pltpu.VMEM((8, 4, 48, 128), BF16),
            pltpu.VMEM((4, 8, 24, 128), BF16),
            pltpu.VMEM((8, 4, 24, 128), BF16),
            pltpu.VMEM((8, 128, 512), BF16),
            pltpu.VMEM((8, 512, 192), BF16),
            pltpu.VMEM((64, 128), F32),
            pltpu.VMEM((64, 128), F32),
            dma((2,)), dma((2,)), dma((2,)), dma((2,)),
            dma, dma, dma, dma,
            dma, dma((4,)),
            dma, dma, dma, dma,
            dma, dma, dma, dma,
            dma, dma, dma, dma, dma, dma,
            dma((3,)),
            *[pltpu.VMEM(a.shape, a.dtype) for a in operands],
            dma((1 + len(operands),)),
        ],
        compiler_params=pltpu.CompilerParams(collective_id=0, has_side_effects=True, vmem_limit_bytes=63 * 1024 * 1024),
    )(tokens, filters.reshape(64, 128), *operands)
    input_grad, weight_grad, filter_grad = pl.pallas_call(
        hand_over,
        out_shape=shapes,
        in_specs=[hbm] * 3,
        out_specs=(hbm, hbm, hbm),
        scratch_shapes=[*[pltpu.VMEM(a.shape, a.dtype) for a in shapes], dma((6,))],
        compiler_params=pltpu.CompilerParams(vmem_limit_bytes=63 * 1024 * 1024),
    )(*made)
    return input_grad, weight_grad.transpose(1, 0, 2), filter_grad.reshape(1, 1, LENGTH)


def solution(mesh):
    placed = (P("ctx", "tp"), P("tp", None, None), P("ctx", "tp"), P("tp", "ctx", None))
    return jax.shard_map(
        on_device,
        mesh=mesh,
        in_specs=placed,
        out_specs=(P("ctx", "tp"), P("ctx", None, "tp"), P("tp", "ctx", None)),
        check_vma=False,
    )
```
